512 devices in a mesh: dp: 128 (over z_lo, x, y), mp: 4 (over z_hi, core).
Axes of the slice: x: 4, y: 4, z: 16 (z_hi: 2, z_lo: 8; z = z_hi * 8 + z_lo), core: 2. Of those that a mesh axis runs over, the one named last changes fastest.
Arguments:
- acts: bfloat16 [65536, 4608], P('dp', 'mp'), may hold values from -6 to 6
- cotangent: bfloat16 [65536, 2048], P('dp', 'mp'), may hold values from -6 to 6
- lengths: int32 [128, 8], P('dp'), may hold values from 1 to 64, as said below
- policy: int32 [128, 8], P('dp'), may hold values from 0 to 7
- advantages: float32 [128, 8], P('dp'), may hold values from -4 to 4
- sampler_log_prob: float32 [65536], P('dp'), may hold values from -4 to -0.5
- current_log_prob: float32 [65536], P('dp'), may hold values from -4 to -0.5
- down_factors: bfloat16 [4608, 512], P('mp'), may hold values from -0.09375 to 0.09375
- up_factors: bfloat16 [512, 2048], P(None, 'mp'), may hold values from -0.125 to 0.125
Outputs:
- grad_a: float32 [512, 4608], P('dp', 'mp')
- grad_b: float32 [512, 2048], P('dp', 'mp')
The draws below stay inside these ranges and needn't reach their ends.
Inputs may be any that keep to these rules, and one draw needn't show every extreme that they name: `lengths`: each row sums to 512 or less, some row to exactly 512; the largest entry is exactly 64.
All inputs are finite; a program needn't handle non-finite values.
Results may differ from the reference program's by a relative error of at most 0.0005.
Values may be sent and summed in bfloat16 or wider, within the bound.
No kernel may reach another device: no remote copies, remote signals or barrier semaphores. Data moves between devices by JAX's collectives and lax.ppermute only.
A program may use at most 64 MiB of HBM per device.

```python
import jax
import jax.numpy as jnp
from jax import lax

MODEL_WIDTH = 4608
VALUE_WIDTH = 2048
ADAPTER_RANK = 64
POLICY_TOTAL = 8
SEQ = 8
MOST = 64
TOKENS = 65536
N_DP = 128


def draw_lengths(key, part):
    key = jax.random.fold_in(key, 11)
    bit_key, len_key = jax.random.split(key)
    index = jnp.arange(N_DP, dtype=jnp.int32)
    bits = jax.random.randint(bit_key, (N_DP,), 0, 2).astype(jnp.int32)
    bits = jnp.where(index == 0, 1, jnp.where(index == N_DP - 1, 0, bits)).astype(jnp.int32)
    before = jnp.roll(bits, 1)
    heavy = (bits * (1 - before)).astype(jnp.int32)
    fed = jnp.roll(heavy, 1)
    slot = jnp.arange(SEQ, dtype=jnp.int32)[None, :]
    heavy_b = heavy[:, None] == 1
    fed_b = fed[:, None] == 1
    low = jnp.where(heavy_b, jnp.where(slot < SEQ - 2, 3 * MOST // 4, MOST // 2), 1)
    high = jnp.where(heavy_b, MOST, jnp.where(fed_b, MOST // 2, 3 * MOST // 4))
    low = jnp.broadcast_to(low, (N_DP, SEQ)).astype(jnp.int32)
    high = jnp.broadcast_to(high, (N_DP, SEQ)).astype(jnp.int32)
    drawn = jax.random.randint(len_key, (N_DP, SEQ), low, high + 1).astype(jnp.int32)
    forced = (index == 0)[:, None]
    return jnp.where(forced, MOST, drawn).astype(jnp.int32)


def touch_ends(result, stream_key, low, largest):
    spot = [jax.random.randint(jax.random.fold_in(stream_key, axis), (), 0, length) for axis, length in enumerate(result.shape)]
    main_axis = result.shape.index(max(result.shape))
    next_to = spot[:main_axis] + [(spot[main_axis] + 1) % result.shape[main_axis]] + spot[main_axis + 1:]
    return result.at[tuple(spot)].set(low).at[tuple(next_to)].set(largest)


def shard_levels(key, extent, cuts, least, largest):
    def one(axis_at, parts):
        steps = jax.random.uniform(jax.random.fold_in(jax.random.fold_in(key, 6), axis_at), (parts,), jnp.float32, least / len(cuts), largest / len(cuts))
        return jnp.repeat(jnp.exp(steps), extent[axis_at] // parts).reshape((-1,) + (1,) * (len(extent) - axis_at - 1))

    loudness = one(*cuts[0])
    for cut in cuts[1:]:
        loudness = loudness * one(*cut)
    return loudness


def gaussian(rng, dims, scale, bound, cuts=(), held_as=jnp.bfloat16):
    level = shard_levels(rng, dims, cuts, -0.22, 0.18) if cuts else 1.0
    result = jax.random.normal(rng, dims, jnp.float32) * scale * level
    return jnp.minimum(jnp.maximum(result, -bound), bound).astype(held_as)


def setup_inputs(seed: int = 0) -> dict:
    key_of = jax.random.split(jax.random.key(seed), 10)
    acts = gaussian(key_of[0], (TOKENS, MODEL_WIDTH), 1.0, 6.0, ((0, 128), (1, 4)))
    cotangent = gaussian(key_of[1], (TOKENS, VALUE_WIDTH), 1.0, 6.0, ((0, 128), (1, 4)))
    lengths = draw_lengths(jax.random.fold_in(key_of[9], 71), 0)
    policy = touch_ends(jax.random.randint(key_of[3], (N_DP, SEQ), 0, POLICY_TOTAL), jax.random.fold_in(key_of[3], 1), 0, POLICY_TOTAL - 1).astype(jnp.int32)
    advantages = gaussian(key_of[4], (N_DP, SEQ), 1.0, 4.0, ((0, 128),), jnp.float32)
    sampler_log_prob = jnp.clip(-4.0 + 3.5 * jax.random.uniform(key_of[5], (TOKENS,), jnp.float32) ** shard_levels(key_of[5], (TOKENS,), ((0, 128),), -0.2, 0.2), -4.0, -0.5)
    current_log_prob = jnp.clip(-4.0 + 3.5 * jax.random.uniform(key_of[6], (TOKENS,), jnp.float32) ** shard_levels(key_of[6], (TOKENS,), ((0, 128),), -0.2, 0.2), -4.0, -0.5)
    down_factors = gaussian(key_of[7], (MODEL_WIDTH, POLICY_TOTAL * ADAPTER_RANK), MODEL_WIDTH ** -0.5, 0.09375, ((0, 4),))
    up_factors = gaussian(key_of[8], (POLICY_TOTAL * ADAPTER_RANK, VALUE_WIDTH), VALUE_WIDTH ** -0.5, 0.125, ((1, 4),))
    return {"acts": acts, "cotangent": cotangent, "lengths": lengths, "policy": policy, "advantages": advantages, "sampler_log_prob": sampler_log_prob, "current_log_prob": current_log_prob, "down_factors": down_factors, "up_factors": up_factors}


ADAPTER_SCALE = 2.0
CLIP_LOW = 0.8
CLIP_HIGH = 1.28


def copy_terms(acts, cotangent, lengths, policy, advantages, sampler_log_prob, current_log_prob, down_factors, up_factors):
    capacity = acts.shape[0]
    seq_count = lengths.shape[0]
    number_policies = down_factors.shape[1] // ADAPTER_RANK
    bounds = jnp.cumsum(lengths).astype(jnp.int32)
    position = jnp.arange(capacity, dtype=jnp.int32)
    seq_of = jnp.sum((position[:, None] >= bounds[None, :]).astype(jnp.int32), axis=1)
    policy_member = (seq_of[:, None] == jnp.arange(seq_count, dtype=jnp.int32)[None, :])
    sequence_totals = advantages / lengths.astype(jnp.float32)
    probability_ratios = jnp.clip(jnp.exp(current_log_prob - sampler_log_prob), CLIP_LOW, CLIP_HIGH)
    frozen_weight = ADAPTER_SCALE * jnp.sum(jnp.where(policy_member, sequence_totals[None, :], jnp.float32(0.0)), axis=1) * probability_ratios
    token_policy = jnp.sum(policy_member.astype(jnp.int32) * policy[None, :], axis=1).astype(jnp.int32)
    owners = (token_policy[:, None] == jnp.arange(number_policies, dtype=jnp.int32)[None, :]).astype(jnp.float32)
    spread = jnp.repeat(owners, ADAPTER_RANK, axis=1)
    reduced_input = jnp.dot(acts, down_factors, preferred_element_type=jnp.float32)
    reduced_output = jnp.dot(cotangent, up_factors.T, preferred_element_type=jnp.float32)
    in_own = jnp.sum(reduced_input.reshape(capacity, number_policies, ADAPTER_RANK) * owners[:, :, None], axis=1)
    out_own = jnp.sum(reduced_output.reshape(capacity, number_policies, ADAPTER_RANK) * owners[:, :, None], axis=1)
    hidden_w = frozen_weight[:, None] * in_own
    grad_w = frozen_weight[:, None] * out_own
    hidden_wide = jnp.tile(hidden_w, (1, number_policies)) * spread
    grad_wide = jnp.tile(grad_w, (1, number_policies)) * spread
    down_term = jnp.dot(grad_wide.T, acts.astype(jnp.float32), precision=lax.Precision.HIGHEST, preferred_element_type=jnp.float32)
    up_term = jnp.dot(hidden_wide.T, cotangent.astype(jnp.float32), precision=lax.Precision.HIGHEST, preferred_element_type=jnp.float32)
    return down_term, up_term


def reference(acts, cotangent, lengths, policy, advantages, sampler_log_prob, current_log_prob, down_factors, up_factors):
    replicas = lengths.shape[0]
    capacity = acts.shape[0] // replicas
    acts_r = acts.reshape(replicas, capacity, acts.shape[1])
    cot_r = cotangent.reshape(replicas, capacity, cotangent.shape[1])
    old_r = sampler_log_prob.reshape(replicas, capacity)
    new_r = current_log_prob.reshape(replicas, capacity)

    def step(carry, entry_list):
        down_term, up_term = copy_terms(entry_list[0], entry_list[1], entry_list[2], entry_list[3], entry_list[4], entry_list[5], entry_list[6], down_factors, up_factors)
        return (carry[0] + down_term, carry[1] + up_term), None

    down_start = jnp.zeros((down_factors.shape[1], acts.shape[1]), jnp.float32)
    up_start = jnp.zeros((up_factors.shape[0], cotangent.shape[1]), jnp.float32)
    totals, unused = lax.scan(step, (down_start, up_start), (acts_r, cot_r, lengths, policy, advantages, old_r, new_r))
    return totals[0], totals[1]
```

```python
import functools

import jax
import jax.numpy as jnp
import numpy as np
from jax import lax
from jax.experimental import pallas as pl
from jax.experimental.pallas import tpu as pltpu
from jax.sharding import PartitionSpec as P

RANK = 64
POLICIES = 8
SEQS = 8
ADAPTER_SCALE = 2.0
CLIP_LOW = 0.8
CLIP_HIGH = 1.28
TINY = 1e-30
TOP = 32767.0
F32, BF16, I16, I32 = jnp.float32, jnp.bfloat16, jnp.int16, jnp.int32
BOTH = ("dp", "mp")
VMEM = pl.BlockSpec(memory_space=pltpu.VMEM)
SMEM = pl.BlockSpec(memory_space=pltpu.SMEM)


def code_of(largest):
    return jnp.ceil(jnp.log2(jnp.maximum(largest, TINY)) * 256.0) + 1.0


def scale_of(code):
    return jnp.exp2(code * (1.0 / 256.0))


def to_i16(values):
    return jnp.clip(jnp.round(values), -TOP, TOP).astype(I32).astype(I16)


def from_i16(values):
    return values.astype(I32).astype(F32)


def starts_of(lengths_ref):
    bounds = [jnp.int32(0)]
    for s in range(SEQS):
        bounds.append(bounds[-1] + lengths_ref[0, s])
    return bounds


def low_kernel(
    lengths_ref, policy_ref, adv_ref, old_ref, new_ref, acts_ref, cot_ref, down_ref, up_ref, keep_ref, send_ref, x_ref
):
    tokens = acts_ref.shape[0]
    half = tokens // 2
    bounds = starts_of(lengths_ref)
    row = lax.broadcasted_iota(I32, (tokens, 128), 0)
    lane = lax.broadcasted_iota(I32, (tokens, 128), 1)
    owner = jnp.full((tokens, 128), -1, I32)
    factor = jnp.zeros((tokens, 128), F32)
    for s in range(SEQS):
        inside = (row >= bounds[s]) & (row < bounds[s + 1])
        total = jnp.full((8, 128), adv_ref[0, s], F32) / jnp.full((8, 128), lengths_ref[0, s], I32).astype(F32)
        owner = jnp.where(inside, policy_ref[0, s], owner)
        factor = jnp.where(inside, total[0:1, :], factor)
    ratio = jnp.clip(jnp.exp(new_ref[...] - old_ref[...]), CLIP_LOW, CLIP_HIGH) * ADAPTER_SCALE
    groups = ratio.shape[0]
    ratio = jnp.concatenate([ratio, jnp.zeros((128 - groups, 128), F32)], axis=0).T
    ratio = jnp.concatenate([ratio[:, j : j + 1] for j in range(groups)], axis=0)
    weight = factor * ratio

    def own(full):
        total = jnp.zeros((tokens, 128), F32)
        for j in range(POLICIES // 2):
            mine = owner == 2 * j + jnp.where(lane >= RANK, 1, 0)
            total = total + jnp.where(mine, full[:, j * 128 : (j + 1) * 128], 0.0)
        return total + pltpu.roll(total, RANK, 1)

    low_in = own(jnp.dot(acts_ref[...], down_ref[...], preferred_element_type=F32))
    low_out = own(
        lax.dot_general(cot_ref[...], up_ref[...], (((1,), (1,)), ((), ())), preferred_element_type=F32)
    )
    x_ref[...] = jnp.where(lane < RANK, low_in, low_out) * weight
    core = lax.rem(lax.axis_index("mp"), 2)
    keep_ref[...] = x_ref[pl.ds(pl.multiple_of(core * half, half), half), :]
    send_ref[...] = x_ref[pl.ds(pl.multiple_of((1 - core) * half, half), half), :]


BLOCKS = 4


def pack_kernel(keep_ref, got_ref, sum_ref, out_ref):
    half = keep_ref.shape[0]
    step = half // BLOCKS
    total = keep_ref[...] + got_ref[...]
    sum_ref[...] = total
    codes = []
    for b in range(BLOCKS):
        part = total[b * step : (b + 1) * step]
        code = code_of(jnp.max(jnp.abs(part), axis=0, keepdims=True))
        codes.append(code)
        out_ref[b * step : (b + 1) * step, :] = to_i16(part * (TOP / scale_of(code)))
    codes.append(jnp.zeros((16 - BLOCKS, 128), F32))
    out_ref[half:, :] = jnp.concatenate(codes, axis=0).astype(I32).astype(I16)


def unpack_kernel(sum_ref, got_ref, out_ref):
    half = sum_ref.shape[0]
    step = half // BLOCKS
    scale = scale_of(from_i16(got_ref[half:, :])) * (1.0 / TOP)
    for b in range(BLOCKS):
        at = slice(b * step, (b + 1) * step)
        out_ref[at, :] = sum_ref[at, :] + from_i16(got_ref[at, :]) * scale[b : b + 1]


def quantize(values_a, values_b, width_a):
    code_a = code_of(jnp.max(jnp.abs(values_a), axis=1, keepdims=True))
    code_b = code_of(jnp.max(jnp.abs(values_b), axis=1, keepdims=True))
    lane = lax.broadcasted_iota(I32, (values_a.shape[0], 128), 1)
    codes = jnp.where(lane < 64, code_a, code_b)
    inverse = TOP / scale_of(codes)
    q_a = to_i16(values_a * inverse[:, 0:1])
    q_b = to_i16(values_b * inverse[:, 64:65])
    return q_a, q_b, codes.astype(I32).astype(I16)


def grad_kernel(lengths_ref, policy_ref, mine_ref, other_ref, acts_ref, cot_ref, out_ref, full_ref, fa_ref, fb_ref):
    tokens, wide_a = acts_ref.shape
    wide_b = cot_ref.shape[1]
    half = tokens // 2
    core = lax.rem(lax.axis_index("mp"), 2)
    full_ref[pl.ds(pl.multiple_of(core * half, half), half), :] = mine_ref[...]
    full_ref[pl.ds(pl.multiple_of((1 - core) * half, half), half), :] = other_ref[...]
    low = full_ref[...].T
    bounds = starts_of(lengths_ref)
    pos = lax.broadcasted_iota(I32, (POLICIES * 4, tokens), 1)
    member = lax.broadcasted_iota(I32, (POLICIES * 4, tokens), 0) // 4
    owner = jnp.full((POLICIES * 4, tokens), -1, I32)
    for s in range(SEQS):
        owner = jnp.where((pos >= bounds[s]) & (pos < bounds[s + 1]), policy_ref[0, s], owner)
    mask = owner == member

    def wide(rows):
        groups = []
        for k in range(4):
            for d in range(4):
                first = rows[k * 16 + d * 4 : k * 16 + d * 4 + 4]
                second = rows[d * 16 + k * 4 : d * 16 + k * 4 + 4]
                part = jnp.where(core == 0, first, second)
                part = jnp.concatenate([part] * POLICIES, axis=0)
                groups.append(jnp.where(mask, part, 0.0))
        both = jnp.concatenate(groups, axis=0)
        high = both.astype(BF16)
        return high, (both - high.astype(F32)).astype(BF16)

    for rows, x_ref, f_ref in ((low[RANK:], acts_ref, fa_ref), (low[:RANK], cot_ref, fb_ref)):
        high, rest = wide(rows)
        width = x_ref.shape[1]
        for c0 in range(0, width, 256):
            c1 = min(c0 + 256, width)
            x = x_ref[:, c0:c1]
            f_ref[:, c0:c1] = jnp.dot(high, x, preferred_element_type=F32) + jnp.dot(
                rest, x, preferred_element_type=F32
            )
    step = out_ref.shape[1]
    for k in range(4):
        at = slice(k * step, (k + 1) * step)
        q_a, q_b, codes = quantize(fa_ref[at, :], fb_ref[at, :], wide_a)
        out_ref[k, :, :wide_a] = q_a
        out_ref[k, :, wide_a : wide_a + wide_b] = q_b
        out_ref[k, :, wide_a + wide_b :] = codes


def sum_parts(got_ref, wide_a, wide_b):
    total_a = total_b = None
    for k in range(got_ref.shape[0]):
        scale = scale_of(from_i16(got_ref[k, :, wide_a + wide_b :])) * (1.0 / TOP)
        a = from_i16(got_ref[k, :, :wide_a]) * scale[:, 0:1]
        b = from_i16(got_ref[k, :, wide_a : wide_a + wide_b]) * scale[:, 64:65]
        total_a = a if total_a is None else total_a + a
        total_b = b if total_b is None else total_b + b
    return total_a, total_b


def second_kernel(wide_a, wide_b, got_ref, out_ref):
    total_a, total_b = sum_parts(got_ref, wide_a, wide_b)
    q_a, q_b, codes = quantize(total_a, total_b, wide_a)
    rows = out_ref.shape[1]
    for k in range(4):
        at = slice(k * rows, (k + 1) * rows)
        out_ref[k, :, :wide_a] = q_a[at]
        out_ref[k, :, wide_a : wide_a + wide_b] = q_b[at]
        out_ref[k, :, wide_a + wide_b :] = codes[at]


def third_kernel(wide_a, wide_b, got_ref, out_ref):
    total_a, total_b = sum_parts(got_ref, wide_a, wide_b)
    for p in range(POLICIES):
        a = total_a[p * 4 : (p + 1) * 4]
        b = total_b[p * 4 : (p + 1) * 4]
        code_a = code_of(jnp.max(jnp.abs(a)).reshape(1, 1))
        code_b = code_of(jnp.max(jnp.abs(b)).reshape(1, 1))
        pieces = [a[:, c : c + 128] * (TOP / scale_of(code_a)) for c in range(0, wide_a, 128)]
        pieces += [b[:, c : c + 128] * (TOP / scale_of(code_b)) for c in range(0, wide_b, 128)]
        pieces.append(jnp.broadcast_to(code_a, (4, 128)))
        pieces.append(jnp.broadcast_to(code_b, (4, 128)))
        pieces.append(jnp.zeros((4, 128), F32))
        out_ref[p] = to_i16(jnp.concatenate(pieces, axis=0))


def last_kernel(wide_a, wide_b, got_ref, a_ref, b_ref):
    n_a, n_b = wide_a // 128, wide_b // 128
    total = None
    for k in range(POLICIES):
        values = from_i16(got_ref[k])
        at = 4 * (n_a + n_b)
        s_a = scale_of(values[at : at + 1]) * (1.0 / TOP)
        s_b = scale_of(values[at + 4 : at + 5]) * (1.0 / TOP)
        row = lax.broadcasted_iota(I32, values.shape, 0)
        values = values * jnp.where(row < 4 * n_a, s_a, s_b)
        total = values if total is None else total + values
    for c in range(n_a):
        a_ref[:, c * 128 : (c + 1) * 128] = total[c * 4 : (c + 1) * 4]
    for c in range(n_b):
        b_ref[:, c * 128 : (c + 1) * 128] = total[4 * (n_a + c) : 4 * (n_a + c + 1)]


def call(kernel, outs, n_smem, n_vmem, scratch=(), flops=0):
    return pl.pallas_call(
        kernel,
        out_shape=[jax.ShapeDtypeStruct(s, d) for s, d in outs],
        in_specs=[SMEM] * n_smem + [VMEM] * n_vmem,
        out_specs=[VMEM] * len(outs),
        scratch_shapes=[pltpu.VMEM(s, d) for s, d in scratch],
        compiler_params=pltpu.CompilerParams(vmem_limit_bytes=40 * 1024 * 1024),
    )


def groups_of():
    index = np.arange(512).reshape(8, 4, 4, 2, 2)
    first, second = [], []
    for z in range(8):
        for h in range(2):
            for k in range(4):
                first.append(index[z, :, k, h, 0].tolist())
                first.append(index[z, k, :, h, 1].tolist())
                second.append(index[z, k, :, h, 0].tolist())
                second.append(index[z, :, k, h, 1].tolist())
    third = [index[:, x, y, h, c].tolist() for x in range(4) for y in range(4) for h in range(2) for c in range(2)]
    return first, second, third


def shards(acts, cot, lengths, policy, advantages, old, new, down, up):
    tokens, wide_a = acts.shape
    wide_b = cot.shape[1]
    half = tokens // 2
    first, second, third = groups_of()
    core_pairs = [(0, 1), (1, 0), (2, 3), (3, 2)]
    far_pairs = [(0, 2), (2, 0), (1, 3), (3, 1)]
    keep, send = call(
        low_kernel, [((half, 128), F32)] * 2, 3, 6, [((tokens, 128), F32)]
    )(lengths, policy, advantages, old.reshape(tokens // 128, 128), new.reshape(tokens // 128, 128), acts, cot, down, up)
    got = lax.ppermute(send, "mp", core_pairs)
    part, packed = call(pack_kernel, [((half, 128), F32), ((half + 16, 128), I16)], 0, 2)(keep, got)
    far = lax.ppermute(packed, "mp", far_pairs)
    (mine,) = call(unpack_kernel, [((half, 128), F32)], 0, 2)(part, far)
    other = lax.ppermute(mine, "mp", core_pairs)
    rows = POLICIES * RANK
    width = wide_a + wide_b + 128
    (pieces,) = call(
        grad_kernel,
        [((4, rows // 4, width), I16)],
        2,
        4,
        [((tokens, 128), F32), ((rows, wide_a), F32), ((rows, wide_b), F32)],
    )(lengths, policy, mine, other, acts, cot)
    got = lax.all_to_all(pieces, BOTH, 0, 0, tiled=True, axis_index_groups=first)
    (pieces,) = call(
        functools.partial(second_kernel, wide_a, wide_b), [((4, rows // 16, width), I16)], 0, 1
    )(got)
    got = lax.all_to_all(pieces, BOTH, 0, 0, tiled=True, axis_index_groups=second)
    deep = 4 * (wide_a + wide_b) // 128 + 12
    (pieces,) = call(
        functools.partial(third_kernel, wide_a, wide_b), [((POLICIES, deep, 128), I16)], 0, 1
    )(got)
    got = lax.all_to_all(pieces, BOTH, 0, 0, tiled=True, axis_index_groups=third)
    return tuple(
        call(
            functools.partial(last_kernel, wide_a, wide_b), [((4, wide_a), F32), ((4, wide_b), F32)], 0, 1
        )(got)
    )


def solution(mesh):
    return jax.shard_map(
        shards,
        mesh=mesh,
        in_specs=(
            P("dp", "mp"),
            P("dp", "mp"),
            P("dp", None),
            P("dp", None),
            P("dp", None),
            P("dp"),
            P("dp"),
            P("mp", None),
            P(None, "mp"),
        ),
        out_specs=(P("dp", "mp"), P("dp", "mp")),
        check_vma=False,
    )
```

```python
import functools

import jax
import jax.numpy as jnp
import numpy as np
from jax import lax
from jax.experimental import pallas as pl
from jax.experimental.pallas import tpu as pltpu
from jax.sharding import PartitionSpec as P

RANK = 64
POLICIES = 8
SEQS = 8
ADAPTER_SCALE = 2.0
CLIP_LOW = 0.8
CLIP_HIGH = 1.28
TINY = 1e-30
TOP = 32767.0
F32, BF16, I16, I32 = jnp.float32, jnp.bfloat16, jnp.int16, jnp.int32
BOTH = ("dp", "mp")
VMEM, SMEM, HBM = pltpu.VMEM, pltpu.SMEM, pltpu.HBM


def code_of(largest):
    return jnp.ceil(jnp.log2(jnp.maximum(largest, TINY)) * 256.0) + 1.0


def scale_of(code):
    return jnp.exp2(code * (1.0 / 256.0))


def to_i16(values):
    return jnp.round(values).astype(I32).astype(I16)


def from_i16(values):
    return values.astype(I32).astype(F32)


def starts_of(lengths_ref):
    bounds = [jnp.int32(0)]
    for s in range(SEQS):
        bounds.append(bounds[-1] + lengths_ref[0, s])
    return bounds


CUT = 512


def low_kernel(
    lengths_hbm, policy_hbm, adv_hbm, old_hbm, new_hbm, acts_hbm, cot_hbm, down_hbm, up_hbm,
    keep_ref, send_ref,
    x_ref, lengths_ref, policy_ref, adv_ref, old_ref, new_ref, acts_ref, cot_ref, down_ref, up_ref, sems,
):
    tokens, wide_a = acts_ref.shape
    half = tokens // 2
    pairs = [
        (lengths_hbm, lengths_ref),
        (policy_hbm, policy_ref),
        (adv_hbm, adv_ref),
        (old_hbm, old_ref),
        (new_hbm, new_ref),
        (cot_hbm, cot_ref),
        (up_hbm, up_ref),
        (acts_hbm.at[:, :CUT], acts_ref.at[:, :CUT]),
        (down_hbm.at[:CUT, :], down_ref.at[:CUT, :]),
        (acts_hbm.at[:, CUT:], acts_ref.at[:, CUT:]),
        (down_hbm.at[CUT:, :], down_ref.at[CUT:, :]),
    ]
    copies = [pltpu.make_async_copy(src, dst, sems.at[i]) for i, (src, dst) in enumerate(pairs)]
    for copy in copies:
        copy.start()
    for copy in copies[:5]:
        copy.wait()
    bounds = starts_of(lengths_ref)
    row = lax.broadcasted_iota(I32, (tokens, 128), 0)
    lane = lax.broadcasted_iota(I32, (tokens, 128), 1)
    owner = jnp.full((tokens, 128), -1, I32)
    factor = jnp.zeros((tokens, 128), F32)
    for s in range(SEQS):
        inside = (row >= bounds[s]) & (row < bounds[s + 1])
        total = jnp.full((8, 128), adv_ref[0, s], F32) / jnp.full((8, 128), lengths_ref[0, s], I32).astype(F32)
        owner = jnp.where(inside, policy_ref[0, s], owner)
        factor = jnp.where(inside, total[0:1, :], factor)
    ratio = jnp.clip(jnp.exp(new_ref[...] - old_ref[...]), CLIP_LOW, CLIP_HIGH) * ADAPTER_SCALE
    groups = ratio.shape[0]
    ratio = jnp.concatenate([ratio, jnp.zeros((128 - groups, 128), F32)], axis=0).T
    ratio = jnp.concatenate([ratio[:, j : j + 1] for j in range(groups)], axis=0)
    weight = factor * ratio

    def own(full):
        total = jnp.zeros((tokens, 128), F32)
        for j in range(POLICIES // 2):
            mine = owner == 2 * j + jnp.where(lane >= RANK, 1, 0)
            total = total + jnp.where(mine, full[:, j * 128 : (j + 1) * 128], 0.0)
        return total + pltpu.roll(total, RANK, 1)

    copies[5].wait()
    copies[6].wait()
    low_out = own(
        lax.dot_general(cot_ref[...], up_ref[...], (((1,), (1,)), ((), ())), preferred_element_type=F32)
    )
    copies[7].wait()
    copies[8].wait()
    low_in = jnp.dot(acts_ref[:, :CUT], down_ref[:CUT, :], preferred_element_type=F32)
    copies[9].wait()
    copies[10].wait()
    low_in = own(low_in + jnp.dot(acts_ref[:, CUT:], down_ref[CUT:, :], preferred_element_type=F32))
    x_ref[...] = jnp.where(lane < RANK, low_in, low_out) * weight
    core = lax.rem(lax.axis_index("mp"), 2)
    keep_ref[...] = x_ref[pl.ds(pl.multiple_of(core * half, half), half), :]
    send_ref[...] = x_ref[pl.ds(pl.multiple_of((1 - core) * half, half), half), :]


BLOCKS = 4


def pack_kernel(keep_ref, got_ref, sum_ref, out_ref):
    half = keep_ref.shape[0]
    step = half // BLOCKS
    total = keep_ref[...] + got_ref[...]
    sum_ref[...] = total
    codes = []
    for b in range(BLOCKS):
        part = total[b * step : (b + 1) * step]
        code = code_of(jnp.max(jnp.abs(part), axis=0, keepdims=True))
        codes.append(code)
        out_ref[b * step : (b + 1) * step, :] = to_i16(part * (TOP / scale_of(code)))
    codes.append(jnp.zeros((16 - BLOCKS, 128), F32))
    out_ref[half:, :] = jnp.concatenate(codes, axis=0).astype(I32).astype(I16)


def unpack_kernel(sum_ref, got_ref, out_ref):
    half = sum_ref.shape[0]
    step = half // BLOCKS
    scale = scale_of(from_i16(got_ref[half:, :])) * (1.0 / TOP)
    for b in range(BLOCKS):
        at = slice(b * step, (b + 1) * step)
        out_ref[at, :] = sum_ref[at, :] + from_i16(got_ref[at, :]) * scale[b : b + 1]


def quantize(values_a, values_b, width_a):
    code_a = code_of(jnp.max(jnp.abs(values_a), axis=1, keepdims=True))
    code_b = code_of(jnp.max(jnp.abs(values_b), axis=1, keepdims=True))
    lane = lax.broadcasted_iota(I32, (values_a.shape[0], 128), 1)
    codes = jnp.where(lane < 64, code_a, code_b)
    inverse = TOP / scale_of(codes)
    q_a = to_i16(values_a * inverse[:, 0:1])
    q_b = to_i16(values_b * inverse[:, 64:65])
    return q_a, q_b, codes.astype(I32).astype(I16)


def grad_kernel(lengths_ref, policy_ref, mine_ref, other_ref, acts_ref, cot_ref, out_ref, full_ref, fa_ref, fb_ref):
    tokens, wide_a = acts_ref.shape
    wide_b = cot_ref.shape[1]
    half = tokens // 2
    core = lax.rem(lax.axis_index("mp"), 2)
    full_ref[pl.ds(pl.multiple_of(core * half, half), half), :] = mine_ref[...]
    full_ref[pl.ds(pl.multiple_of((1 - core) * half, half), half), :] = other_ref[...]
    low = full_ref[...].T
    bounds = starts_of(lengths_ref)
    pos = lax.broadcasted_iota(I32, (POLICIES * 4, tokens), 1)
    member = lax.broadcasted_iota(I32, (POLICIES * 4, tokens), 0) // 4
    owner = jnp.full((POLICIES * 4, tokens), -1, I32)
    for s in range(SEQS):
        owner = jnp.where((pos >= bounds[s]) & (pos < bounds[s + 1]), policy_ref[0, s], owner)
    mask = owner == member

    def wide(rows):
        groups = []
        for k in range(4):
            for d in range(4):
                first = rows[k * 16 + d * 4 : k * 16 + d * 4 + 4]
                second = rows[d * 16 + k * 4 : d * 16 + k * 4 + 4]
                part = jnp.where(core == 0, first, second)
                part = jnp.concatenate([part] * POLICIES, axis=0)
                groups.append(jnp.where(mask, part, 0.0))
        both = jnp.concatenate(groups, axis=0)
        high = both.astype(BF16)
        return high, (both - high.astype(F32)).astype(BF16)

    for rows, x_ref, f_ref in ((low[RANK:], acts_ref, fa_ref), (low[:RANK], cot_ref, fb_ref)):
        high, rest = wide(rows)
        width = x_ref.shape[1]
        for c0 in range(0, width, 256):
            c1 = min(c0 + 256, width)
            x = x_ref[:, c0:c1]
            f_ref[:, c0:c1] = jnp.dot(high, x, preferred_element_type=F32) + jnp.dot(
                rest, x, preferred_element_type=F32
            )
    step = out_ref.shape[1]
    for k in range(4):
        at = slice(k * step, (k + 1) * step)
        q_a, q_b, codes = quantize(fa_ref[at, :], fb_ref[at, :], wide_a)
        out_ref[k, :, :wide_a] = q_a
        out_ref[k, :, wide_a : wide_a + wide_b] = q_b
        out_ref[k, :, wide_a + wide_b :] = codes


def sum_parts(got_ref, wide_a, wide_b):
    total_a = total_b = None
    for k in range(got_ref.shape[0]):
        scale = scale_of(from_i16(got_ref[k, :, wide_a + wide_b :])) * (1.0 / TOP)
        a = from_i16(got_ref[k, :, :wide_a]) * scale[:, 0:1]
        b = from_i16(got_ref[k, :, wide_a : wide_a + wide_b]) * scale[:, 64:65]
        total_a = a if total_a is None else total_a + a
        total_b = b if total_b is None else total_b + b
    return total_a, total_b


def second_kernel(wide_a, wide_b, got_ref, out_ref):
    total_a, total_b = sum_parts(got_ref, wide_a, wide_b)
    q_a, q_b, codes = quantize(total_a, total_b, wide_a)
    rows = out_ref.shape[1]
    for k in range(4):
        at = slice(k * rows, (k + 1) * rows)
        out_ref[k, :, :wide_a] = q_a[at]
        out_ref[k, :, wide_a : wide_a + wide_b] = q_b[at]
        out_ref[k, :, wide_a + wide_b :] = codes[at]


def third_kernel(wide_a, wide_b, got_ref, out_ref):
    total_a, total_b = sum_parts(got_ref, wide_a, wide_b)
    for p in range(POLICIES):
        a = total_a[p * 4 : (p + 1) * 4]
        b = total_b[p * 4 : (p + 1) * 4]
        code_a = code_of(jnp.max(jnp.abs(a)).reshape(1, 1))
        code_b = code_of(jnp.max(jnp.abs(b)).reshape(1, 1))
        pieces = [a[:, c : c + 128] * (TOP / scale_of(code_a)) for c in range(0, wide_a, 128)]
        pieces += [b[:, c : c + 128] * (TOP / scale_of(code_b)) for c in range(0, wide_b, 128)]
        pieces.append(jnp.broadcast_to(code_a, (4, 128)))
        pieces.append(jnp.broadcast_to(code_b, (4, 128)))
        pieces.append(jnp.zeros((4, 128), F32))
        out_ref[p] = to_i16(jnp.concatenate(pieces, axis=0))


def last_kernel(wide_a, wide_b, got_ref, a_ref, b_ref):
    n_a, n_b = wide_a // 128, wide_b // 128
    total = None
    for k in range(POLICIES):
        values = from_i16(got_ref[k])
        at = 4 * (n_a + n_b)
        s_a = scale_of(values[at : at + 1]) * (1.0 / TOP)
        s_b = scale_of(values[at + 4 : at + 5]) * (1.0 / TOP)
        row = lax.broadcasted_iota(I32, values.shape, 0)
        values = values * jnp.where(row < 4 * n_a, s_a, s_b)
        total = values if total is None else total + values
    for c in range(n_a):
        a_ref[:, c * 128 : (c + 1) * 128] = total[c * 4 : (c + 1) * 4]
    for c in range(n_b):
        b_ref[:, c * 128 : (c + 1) * 128] = total[4 * (n_a + c) : 4 * (n_a + c + 1)]


def call(kernel, outs, spaces, scratch=()):
    return pl.pallas_call(
        kernel,
        out_shape=[jax.ShapeDtypeStruct(s, d) for s, d in outs],
        in_specs=[pl.BlockSpec(memory_space=m) for m in spaces],
        out_specs=[pl.BlockSpec(memory_space=pltpu.VMEM)] * len(outs),
        scratch_shapes=list(scratch),
        compiler_params=pltpu.CompilerParams(vmem_limit_bytes=40 * 1024 * 1024),
    )


def in_hbm(array):
    return pltpu.with_memory_space_constraint(array, pltpu.HBM)


def groups_of():
    index = np.arange(512).reshape(8, 4, 4, 2, 2)
    first, second = [], []
    for z in range(8):
        for h in range(2):
            for k in range(4):
                first.append(index[z, :, k, h, 0].tolist())
                first.append(index[z, k, :, h, 1].tolist())
                second.append(index[z, k, :, h, 0].tolist())
                second.append(index[z, :, k, h, 1].tolist())
    third = [index[:, x, y, h, c].tolist() for x in range(4) for y in range(4) for h in range(2) for c in range(2)]
    return first, second, third


def shards(acts, cot, lengths, policy, advantages, old, new, down, up):
    tokens, wide_a = acts.shape
    wide_b = cot.shape[1]
    half = tokens // 2
    first, second, third = groups_of()
    core_pairs = [(0, 1), (1, 0), (2, 3), (3, 2)]
    far_pairs = [(0, 2), (2, 0), (1, 3), (3, 1)]
    lines = (tokens // 128, 128)
    keep, send = call(
        low_kernel,
        [((half, 128), F32)] * 2,
        [HBM] * 9,
        [
            VMEM((tokens, 128), F32),
            SMEM(lengths.shape, I32),
            SMEM(policy.shape, I32),
            SMEM(advantages.shape, F32),
            VMEM(lines, F32),
            VMEM(lines, F32),
            VMEM(acts.shape, BF16),
            VMEM(cot.shape, BF16),
            VMEM(down.shape, BF16),
            VMEM(up.shape, BF16),
            pltpu.SemaphoreType.DMA((11,)),
        ],
    )(*map(in_hbm, (lengths, policy, advantages, old.reshape(lines), new.reshape(lines), acts, cot, down, up)))
    got = lax.ppermute(send, "mp", core_pairs)
    part, packed = call(pack_kernel, [((half, 128), F32), ((half + 16, 128), I16)], [VMEM] * 2)(keep, got)
    far = lax.ppermute(packed, "mp", far_pairs)
    (mine,) = call(unpack_kernel, [((half, 128), F32)], [VMEM] * 2)(part, far)
    other = lax.ppermute(mine, "mp", core_pairs)
    rows = POLICIES * RANK
    width = wide_a + wide_b + 128
    (pieces,) = call(
        grad_kernel,
        [((4, rows // 4, width), I16)],
        [SMEM] * 2 + [VMEM] * 4,
        [VMEM((tokens, 128), F32), VMEM((rows, wide_a), F32), VMEM((rows, wide_b), F32)],
    )(lengths, policy, mine, other, acts, cot)
    got = lax.all_to_all(pieces, BOTH, 0, 0, tiled=True, axis_index_groups=first)
    (pieces,) = call(
        functools.partial(second_kernel, wide_a, wide_b), [((4, rows // 16, width), I16)], [VMEM]
    )(got)
    got = lax.all_to_all(pieces, BOTH, 0, 0, tiled=True, axis_index_groups=second)
    deep = 4 * (wide_a + wide_b) // 128 + 12
    (pieces,) = call(
        functools.partial(third_kernel, wide_a, wide_b), [((POLICIES, deep, 128), I16)], [VMEM]
    )(got)
    got = lax.all_to_all(pieces, BOTH, 0, 0, tiled=True, axis_index_groups=third)
    return tuple(
        call(
            functools.partial(last_kernel, wide_a, wide_b), [((4, wide_a), F32), ((4, wide_b), F32)], [VMEM]
        )(got)
    )


def solution(mesh):
    return jax.shard_map(
        shards,
        mesh=mesh,
        in_specs=(
            P("dp", "mp"),
            P("dp", "mp"),
            P("dp", None),
            P("dp", None),
            P("dp", None),
            P("dp"),
            P("dp"),
            P("mp", None),
            P(None, "mp"),
        ),
        out_specs=(P("dp", "mp"), P("dp", "mp")),
        check_vma=False,
    )
```

```python
import functools

import jax
import jax.numpy as jnp
import numpy as np
from jax import lax
from jax.experimental import pallas as pl
from jax.experimental.pallas import tpu as pltpu
from jax.sharding import PartitionSpec as P

RANK = 64
POLICIES = 8
SEQS = 8
ADAPTER_SCALE = 2.0
CLIP_LOW = 0.8
CLIP_HIGH = 1.28
TINY = 1e-30
TOP = 32767.0
F32, BF16, I16, I32 = jnp.float32, jnp.bfloat16, jnp.int16, jnp.int32
BOTH = ("dp", "mp")
VMEM, SMEM, HBM = pltpu.VMEM, pltpu.SMEM, pltpu.HBM


def code_of(largest):
    return jnp.ceil(jnp.log2(jnp.maximum(largest, TINY)) * 256.0) + 1.0


def scale_of(code):
    return jnp.exp2(code * (1.0 / 256.0))


def to_i16(values):
    return jnp.round(values).astype(I32).astype(I16)


def from_i16(values):
    return values.astype(I32).astype(F32)


def starts_of(lengths_ref):
    bounds = [jnp.int32(0)]
    for s in range(SEQS):
        bounds.append(bounds[-1] + lengths_ref[0, s])
    return bounds


CUT = 512


def low_kernel(
    lengths_hbm, policy_hbm, adv_hbm, old_hbm, new_hbm, acts_hbm, cot_hbm, down_hbm, up_hbm,
    keep_ref, send_ref, owner_ref, acts_ref, cot_ref,
    x_ref, lengths_ref, policy_ref, adv_ref, old_ref, new_ref, down_ref, up_ref, sems,
):
    tokens, wide_a = acts_ref.shape
    half = tokens // 2
    pairs = [
        (lengths_hbm, lengths_ref),
        (policy_hbm, policy_ref),
        (adv_hbm, adv_ref),
        (old_hbm, old_ref),
        (new_hbm, new_ref),
        (cot_hbm, cot_ref),
        (up_hbm, up_ref),
        (acts_hbm.at[:, :CUT], acts_ref.at[:, :CUT]),
        (down_hbm.at[:CUT, :], down_ref.at[:CUT, :]),
        (acts_hbm.at[:, CUT:], acts_ref.at[:, CUT:]),
        (down_hbm.at[CUT:, :], down_ref.at[CUT:, :]),
    ]
    copies = [pltpu.make_async_copy(src, dst, sems.at[i]) for i, (src, dst) in enumerate(pairs)]
    for copy in copies:
        copy.start()
    for copy in copies[:5]:
        copy.wait()
    bounds = starts_of(lengths_ref)
    row = lax.broadcasted_iota(I32, (tokens, 128), 0)
    lane = lax.broadcasted_iota(I32, (tokens, 128), 1)
    owner = jnp.full((tokens, 128), -1, I32)
    factor = jnp.zeros((tokens, 128), F32)
    for s in range(SEQS):
        inside = (row >= bounds[s]) & (row < bounds[s + 1])
        total = jnp.full((8, 128), adv_ref[0, s], F32) / jnp.full((8, 128), lengths_ref[0, s], I32).astype(F32)
        owner = jnp.where(inside, policy_ref[0, s], owner)
        factor = jnp.where(inside, total[0:1, :], factor)
    pos = lax.broadcasted_iota(I32, (POLICIES, tokens), 1)
    held = jnp.full((POLICIES, tokens), -1, I32)
    for s in range(SEQS):
        held = jnp.where((pos >= bounds[s]) & (pos < bounds[s + 1]), policy_ref[0, s], held)
    owner_ref[...] = held
    ratio = jnp.clip(jnp.exp(new_ref[...] - old_ref[...]), CLIP_LOW, CLIP_HIGH) * ADAPTER_SCALE
    groups = ratio.shape[0]
    ratio = jnp.concatenate([ratio, jnp.zeros((128 - groups, 128), F32)], axis=0).T
    ratio = jnp.concatenate([ratio[:, j : j + 1] for j in range(groups)], axis=0)
    weight = factor * ratio

    def own(full):
        total = jnp.zeros((tokens, 128), F32)
        for j in range(POLICIES // 2):
            mine = owner == 2 * j + jnp.where(lane >= RANK, 1, 0)
            total = total + jnp.where(mine, full[:, j * 128 : (j + 1) * 128], 0.0)
        return total + pltpu.roll(total, RANK, 1)

    copies[5].wait()
    copies[6].wait()
    low_out = own(
        lax.dot_general(cot_ref[...], up_ref[...], (((1,), (1,)), ((), ())), preferred_element_type=F32)
    )
    copies[7].wait()
    copies[8].wait()
    low_in = jnp.dot(acts_ref[:, :CUT], down_ref[:CUT, :], preferred_element_type=F32)
    copies[9].wait()
    copies[10].wait()
    low_in = own(low_in + jnp.dot(acts_ref[:, CUT:], down_ref[CUT:, :], preferred_element_type=F32))
    x_ref[...] = jnp.where(lane < RANK, low_in, low_out) * weight
    core = lax.rem(lax.axis_index("mp"), 2)
    keep_ref[...] = x_ref[pl.ds(pl.multiple_of(core * half, half), half), :]
    send_ref[...] = x_ref[pl.ds(pl.multiple_of((1 - core) * half, half), half), :]


BLOCKS = 4


def pack_kernel(keep_ref, got_ref, sum_ref, out_ref):
    half = keep_ref.shape[0]
    step = half // BLOCKS
    total = keep_ref[...] + got_ref[...]
    sum_ref[...] = total
    codes = []
    for b in range(BLOCKS):
        part = total[b * step : (b + 1) * step]
        code = code_of(jnp.max(jnp.abs(part), axis=0, keepdims=True))
        codes.append(code)
        out_ref[b * step : (b + 1) * step, :] = to_i16(part * (TOP / scale_of(code)))
    codes.append(jnp.zeros((16 - BLOCKS, 128), F32))
    out_ref[half:, :] = jnp.concatenate(codes, axis=0).astype(I32).astype(I16)


def unpack_kernel(sum_ref, got_ref, out_ref):
    half = sum_ref.shape[0]
    step = half // BLOCKS
    scale = scale_of(from_i16(got_ref[half:, :])) * (1.0 / TOP)
    for b in range(BLOCKS):
        at = slice(b * step, (b + 1) * step)
        out_ref[at, :] = sum_ref[at, :] + from_i16(got_ref[at, :]) * scale[b : b + 1]


def quantize(values_a, values_b):
    code_a = code_of(jnp.max(jnp.abs(values_a), axis=1, keepdims=True))
    code_b = code_of(jnp.max(jnp.abs(values_b), axis=1, keepdims=True))
    lane = lax.broadcasted_iota(I32, (values_a.shape[0], 128), 1)
    codes = jnp.where(lane == 0, code_a, code_b)
    inverse = TOP / scale_of(codes)
    q_a = to_i16(values_a * inverse[:, 0:1])
    q_b = to_i16(values_b * inverse[:, 1:2])
    return q_a, q_b, codes


def grad_kernel(
    owner_ref, mine_ref, other_ref, acts_ref, cot_ref, out_ref, full_ref, low_ref, left_ref, fa_ref, fb_ref
):
    tokens, wide_a = acts_ref.shape
    wide_b = cot_ref.shape[1]
    half = tokens // 2
    core = lax.rem(lax.axis_index("mp"), 2)
    full_ref[pl.ds(pl.multiple_of(core * half, half), half), :] = mine_ref[...]
    full_ref[pl.ds(pl.multiple_of((1 - core) * half, half), half), :] = other_ref[...]
    low = full_ref[...].T
    high = low.astype(BF16).astype(F32)
    low_ref[0] = high
    low_ref[1] = low - high
    mask = owner_ref[...] == lax.broadcasted_iota(I32, (POLICIES, tokens), 0)

    def spread(side, first_rank):
        for part in range(2):
            for k in range(4):
                for d in range(4):
                    start = first_rank + jnp.where(core == 0, k * 16 + d * 4, d * 16 + k * 4)
                    at = part * 256 + (k % 2) * 128 + d * 32
                    rows = []
                    for i in range(4):
                        row = low_ref[part, pl.ds(start + i, 1), :]
                        rows.append(jnp.where(mask, jnp.broadcast_to(row, mask.shape), 0.0))
                    left_ref[side, k // 2, at : at + 32, :] = jnp.concatenate(rows, axis=0).astype(BF16)

    spread(0, RANK)
    spread(1, 0)
    quarter = full_rows(out_ref, wide_a + wide_b)
    for h in range(2):
        rows = slice(h * 2 * quarter, (h + 1) * 2 * quarter)
        for side, x_ref, f_ref in ((0, acts_ref, fa_ref), (1, cot_ref, fb_ref)):
            left = left_ref[side, h]
            width = x_ref.shape[1]
            for c0 in range(0, width, 256):
                c1 = min(c0 + 256, width)
                both = jnp.dot(left, x_ref[:, c0:c1], preferred_element_type=F32)
                f_ref[rows, c0:c1] = both[: 2 * quarter] + both[2 * quarter :]
        for k in (2 * h, 2 * h + 1):
            at = slice(k * quarter, (k + 1) * quarter)
            q_a, q_b, codes = quantize(fa_ref[at, :], fb_ref[at, :])
            store_columns(out_ref, k, q_a, q_b)
            out_ref[k, -16:, :] = codes.T[:16].astype(I32).astype(I16)


def full_rows(ref, width):
    return (ref.shape[1] - 16) // (width // 128)


def store_columns(out_ref, k, q_a, q_b):
    rows, at = q_a.shape[0], 0
    for q in (q_a, q_b):
        for c in range(0, q.shape[1], 128):
            out_ref[k, at : at + rows, :] = q[:, c : c + 128]
            at += rows


def sum_parts(scales, parts):
    total_a = total_b = None
    for (s_a, s_b), (a, b) in zip(scales, parts):
        a, b = from_i16(a) * s_a, from_i16(b) * s_b
        total_a = a if total_a is None else total_a + a
        total_b = b if total_b is None else total_b + b
    return total_a, total_b


def second_kernel(wide_a, wide_b, got_ref, out_ref):
    rows = full_rows(got_ref, wide_a + wide_b)
    n_a, n_b = wide_a // 128, wide_b // 128
    scales = []
    for k in range(4):
        codes = from_i16(got_ref[k, -16:, :])
        codes = scale_of(jnp.concatenate([codes, jnp.zeros((112, 128), F32)], axis=0).T) * (1.0 / TOP)
        scales.append((codes[:, 0:1], codes[:, 1:2]))

    def column(c):
        total = None
        for k in range(4):
            part = from_i16(got_ref[k, c * rows : (c + 1) * rows, :]) * scales[k][0 if c < n_a else 1]
            total = part if total is None else total + part
        return total

    total_a = jnp.concatenate([column(c) for c in range(n_a)], axis=1)
    total_b = jnp.concatenate([column(c) for c in range(n_a, n_a + n_b)], axis=1)
    q_a, q_b, codes = quantize(total_a, total_b)
    codes = codes.astype(I32).astype(I16)
    rows = out_ref.shape[1]
    for k in range(4):
        at = slice(k * rows, (k + 1) * rows)
        out_ref[k, :, :wide_a] = q_a[at]
        out_ref[k, :, wide_a : wide_a + wide_b] = q_b[at]
        out_ref[k, :, wide_a + wide_b :] = codes[at]


def third_kernel(wide_a, wide_b, got_ref, out_ref, total_ref):
    parts, scales = [], []
    for k in range(4):
        codes = scale_of(from_i16(got_ref[k, :, wide_a + wide_b :])) * (1.0 / TOP)
        scales.append((codes[:, 0:1], codes[:, 1:2]))
        parts.append((got_ref[k, :, :wide_a], got_ref[k, :, wide_a : wide_a + wide_b]))
    total_a, total_b = sum_parts(scales, parts)
    n_a, n_b = wide_a // 128, wide_b // 128
    for c in range(n_a):
        total_ref[c * 32 : (c + 1) * 32, :] = total_a[:, c * 128 : (c + 1) * 128]
    for c in range(n_b):
        total_ref[(n_a + c) * 32 : (n_a + c + 1) * 32, :] = total_b[:, c * 128 : (c + 1) * 128]

    def code_for(parts):
        most = jnp.abs(parts[0])
        for part in parts[1:]:
            most = jnp.maximum(most, jnp.abs(part))
        return code_of(jnp.max(jnp.max(most, axis=0, keepdims=True), axis=1, keepdims=True))

    for p in range(POLICIES):
        parts = [total_ref[pl.ds(c * 32 + p, 4, stride=POLICIES), :] for c in range(n_a + n_b)]
        code_a, code_b = code_for(parts[:n_a]), code_for(parts[n_a:])
        pieces = [part * (TOP / scale_of(code_a)) for part in parts[:n_a]]
        pieces += [part * (TOP / scale_of(code_b)) for part in parts[n_a:]]
        row = lax.broadcasted_iota(I32, (4, 128), 0)
        pieces.append(jnp.where(row == 0, code_a, code_b))
        out_ref[p] = to_i16(jnp.concatenate(pieces, axis=0))


def last_kernel(wide_a, wide_b, got_ref, a_ref, b_ref):
    n_a, n_b = wide_a // 128, wide_b // 128
    total = None
    for k in range(POLICIES):
        values = from_i16(got_ref[k])
        at = 4 * (n_a + n_b)
        s_a = scale_of(values[at : at + 1]) * (1.0 / TOP)
        s_b = scale_of(values[at + 1 : at + 2]) * (1.0 / TOP)
        row = lax.broadcasted_iota(I32, values.shape, 0)
        values = values * jnp.where(row < 4 * n_a, s_a, s_b)
        total = values if total is None else total + values
    for c in range(n_a):
        a_ref[:, c * 128 : (c + 1) * 128] = total[c * 4 : (c + 1) * 4]
    for c in range(n_b):
        b_ref[:, c * 128 : (c + 1) * 128] = total[4 * (n_a + c) : 4 * (n_a + c + 1)]


def call(kernel, outs, spaces, scratch=()):
    return pl.pallas_call(
        kernel,
        out_shape=[jax.ShapeDtypeStruct(s, d) for s, d in outs],
        in_specs=[pl.BlockSpec(memory_space=m) for m in spaces],
        out_specs=[pl.BlockSpec(memory_space=pltpu.VMEM)] * len(outs),
        scratch_shapes=list(scratch),
        compiler_params=pltpu.CompilerParams(vmem_limit_bytes=40 * 1024 * 1024),
    )


def in_hbm(array):
    return pltpu.with_memory_space_constraint(array, pltpu.HBM)


def groups_of():
    index = np.arange(512).reshape(8, 4, 4, 2, 2)
    first, second = [], []
    for z in range(8):
        for h in range(2):
            for k in range(4):
                first.append(index[z, :, k, h, 0].tolist())
                first.append(index[z, k, :, h, 1].tolist())
                second.append(index[z, k, :, h, 0].tolist())
                second.append(index[z, :, k, h, 1].tolist())
    third = [index[:, x, y, h, c].tolist() for x in range(4) for y in range(4) for h in range(2) for c in range(2)]
    return first, second, third


def shards(acts, cot, lengths, policy, advantages, old, new, down, up):
    tokens, wide_a = acts.shape
    wide_b = cot.shape[1]
    half = tokens // 2
    first, second, third = groups_of()
    core_pairs = [(0, 1), (1, 0), (2, 3), (3, 2)]
    far_pairs = [(0, 2), (2, 0), (1, 3), (3, 1)]
    lines = (tokens // 128, 128)
    keep, send, owner, acts, cot = call(
        low_kernel,
        [((half, 128), F32)] * 2 + [((POLICIES, tokens), I32), (acts.shape, BF16), (cot.shape, BF16)],
        [HBM] * 9,
        [
            VMEM((tokens, 128), F32),
            SMEM(lengths.shape, I32),
            SMEM(policy.shape, I32),
            SMEM(advantages.shape, F32),
            VMEM(lines, F32),
            VMEM(lines, F32),
            VMEM(down.shape, BF16),
            VMEM(up.shape, BF16),
            pltpu.SemaphoreType.DMA((11,)),
        ],
    )(*map(in_hbm, (lengths, policy, advantages, old.reshape(lines), new.reshape(lines), acts, cot, down, up)))
    got = lax.ppermute(send, "mp", core_pairs)
    part, packed = call(pack_kernel, [((half, 128), F32), ((half + 16, 128), I16)], [VMEM] * 2)(keep, got)
    far = lax.ppermute(packed, "mp", far_pairs)
    (mine,) = call(unpack_kernel, [((half, 128), F32)], [VMEM] * 2)(part, far)
    other = lax.ppermute(mine, "mp", core_pairs)
    rows = POLICIES * RANK
    width = wide_a + wide_b + 128
    (pieces,) = call(
        grad_kernel,
        [((4, rows // 4 * (wide_a + wide_b) // 128 + 16, 128), I16)],
        [VMEM] * 5,
        [
            VMEM((tokens, 128), F32),
            VMEM((2, 2 * RANK, tokens), F32),
            VMEM((2, 2, rows, tokens), BF16),
            VMEM((rows, wide_a), F32),
            VMEM((rows, wide_b), F32),
        ],
    )(owner, mine, other, acts, cot)
    got = lax.all_to_all(pieces, BOTH, 0, 0, tiled=True, axis_index_groups=first)
    (pieces,) = call(
        functools.partial(second_kernel, wide_a, wide_b), [((4, rows // 16, width), I16)], [VMEM]
    )(got)
    got = lax.all_to_all(pieces, BOTH, 0, 0, tiled=True, axis_index_groups=second)
    deep = 4 * (wide_a + wide_b) // 128 + 4
    (pieces,) = call(
        functools.partial(third_kernel, wide_a, wide_b), [((POLICIES, deep, 128), I16)], [VMEM], [VMEM((rows // 16 * (wide_a + wide_b) // 128, 128), F32)]
    )(got)
    got = lax.all_to_all(pieces, BOTH, 0, 0, tiled=True, axis_index_groups=third)
    return tuple(
        call(
            functools.partial(last_kernel, wide_a, wide_b), [((4, wide_a), F32), ((4, wide_b), F32)], [VMEM]
        )(got)
    )


def solution(mesh):
    return jax.shard_map(
        shards,
        mesh=mesh,
        in_specs=(
            P("dp", "mp"),
            P("dp", "mp"),
            P("dp", None),
            P("dp", None),
            P("dp", None),
            P("dp"),
            P("dp"),
            P("mp", None),
            P(None, "mp"),
        ),
        out_specs=(P("dp", "mp"), P("dp", "mp")),
        check_vma=False,
    )
```

```python
import functools

import jax
import jax.numpy as jnp
import numpy as np
from jax import lax
from jax.experimental import pallas as pl
from jax.experimental.pallas import tpu as pltpu
from jax.sharding import PartitionSpec as P

RANK = 64
POLICIES = 8
SEQS = 8
ADAPTER_SCALE = 2.0
CLIP_LOW = 0.8
CLIP_HIGH = 1.28
TINY = 1e-30
TOP = 32767.0
F32, BF16, I16, I32 = jnp.float32, jnp.bfloat16, jnp.int16, jnp.int32
BOTH = ("dp", "mp")
VMEM, SMEM, HBM = pltpu.VMEM, pltpu.SMEM, pltpu.HBM


def code_of(largest):
    return jnp.ceil(jnp.log2(jnp.maximum(largest, TINY)) * 256.0) + 1.0


def scale_of(code):
    return jnp.exp2(code * (1.0 / 256.0))


def to_i16(values):
    return jnp.round(values).astype(I32).astype(I16)


def from_i16(values):
    return values.astype(I32).astype(F32)


def starts_of(lengths_ref):
    bounds = [jnp.int32(0)]
    for s in range(SEQS):
        bounds.append(bounds[-1] + lengths_ref[0, s])
    return bounds


CUT = 512


def low_kernel(
    lengths_hbm, policy_hbm, adv_hbm, old_hbm, new_hbm, acts_hbm, cot_hbm, down_hbm, up_hbm,
    keep_ref, send_ref, owner_ref, acts_ref, cot_ref,
    x_ref, lengths_ref, policy_ref, adv_ref, old_ref, new_ref, down_ref, up_ref, sems,
):
    tokens, wide_a = acts_ref.shape
    half = tokens // 2
    pairs = [
        (lengths_hbm, lengths_ref),
        (policy_hbm, policy_ref),
        (adv_hbm, adv_ref),
        (old_hbm, old_ref),
        (new_hbm, new_ref),
        (cot_hbm, cot_ref),
        (up_hbm, up_ref),
        (acts_hbm.at[:, :CUT], acts_ref.at[:, :CUT]),
        (down_hbm.at[:CUT, :], down_ref.at[:CUT, :]),
        (acts_hbm.at[:, CUT:], acts_ref.at[:, CUT:]),
        (down_hbm.at[CUT:, :], down_ref.at[CUT:, :]),
    ]
    copies = [pltpu.make_async_copy(src, dst, sems.at[i]) for i, (src, dst) in enumerate(pairs)]
    for copy in copies:
        copy.start()
    for copy in copies[:5]:
        copy.wait()
    bounds = starts_of(lengths_ref)
    row = lax.broadcasted_iota(I32, (tokens, 128), 0)
    lane = lax.broadcasted_iota(I32, (tokens, 128), 1)
    owner = jnp.full((tokens, 128), -1, I32)
    factor = jnp.zeros((tokens, 128), F32)
    for s in range(SEQS):
        inside = (row >= bounds[s]) & (row < bounds[s + 1])
        total = jnp.full((8, 128), adv_ref[0, s], F32) / jnp.full((8, 128), lengths_ref[0, s], I32).astype(F32)
        owner = jnp.where(inside, policy_ref[0, s], owner)
        factor = jnp.where(inside, total[0:1, :], factor)
    pos = lax.broadcasted_iota(I32, (POLICIES, tokens), 1)
    held = jnp.full((POLICIES, tokens), -1, I32)
    for s in range(SEQS):
        held = jnp.where((pos >= bounds[s]) & (pos < bounds[s + 1]), policy_ref[0, s], held)
    owner_ref[...] = held
    ratio = jnp.clip(jnp.exp(new_ref[...] - old_ref[...]), CLIP_LOW, CLIP_HIGH) * ADAPTER_SCALE
    groups = ratio.shape[0]
    ratio = jnp.concatenate([ratio, jnp.zeros((128 - groups, 128), F32)], axis=0).T
    ratio = jnp.concatenate([ratio[:, j : j + 1] for j in range(groups)], axis=0)
    weight = factor * ratio

    def own(full):
        total = jnp.zeros((tokens, 128), F32)
        for j in range(POLICIES // 2):
            mine = owner == 2 * j + jnp.where(lane >= RANK, 1, 0)
            total = total + jnp.where(mine, full[:, j * 128 : (j + 1) * 128], 0.0)
        return total + pltpu.roll(total, RANK, 1)

    copies[5].wait()
    copies[6].wait()
    low_out = own(
        lax.dot_general(cot_ref[...], up_ref[...], (((1,), (1,)), ((), ())), preferred_element_type=F32)
    )
    copies[7].wait()
    copies[8].wait()
    low_in = jnp.dot(acts_ref[:, :CUT], down_ref[:CUT, :], preferred_element_type=F32)
    copies[9].wait()
    copies[10].wait()
    low_in = own(low_in + jnp.dot(acts_ref[:, CUT:], down_ref[CUT:, :], preferred_element_type=F32))
    x_ref[...] = jnp.where(lane < RANK, low_in, low_out) * weight
    core = lax.rem(lax.axis_index("mp"), 2)
    keep_ref[...] = x_ref[pl.ds(pl.multiple_of(core * half, half), half), :]
    send_ref[...] = x_ref[pl.ds(pl.multiple_of((1 - core) * half, half), half), :]


BLOCKS = 4
NEAR = 4


def pack_kernel(keep_ref, got_ref, sum_ref, out_ref):
    half = keep_ref.shape[0]
    step = half // BLOCKS
    total = keep_ref[...] + got_ref[...]
    sum_ref[...] = total
    codes = []
    for b in range(BLOCKS):
        part = total[b * step : (b + 1) * step]
        code = code_of(jnp.max(jnp.abs(part), axis=0, keepdims=True))
        codes.append(code)
        out_ref[b * step : (b + 1) * step, :] = to_i16(part * (TOP / scale_of(code)))
    codes.append(jnp.zeros((16 - BLOCKS, 128), F32))
    out_ref[half:, :] = jnp.concatenate(codes, axis=0).astype(I32).astype(I16)


def unpack_kernel(sum_ref, got_ref, out_ref):
    half = sum_ref.shape[0]
    step = half // BLOCKS
    scale = scale_of(from_i16(got_ref[half:, :])) * (1.0 / TOP)
    for b in range(BLOCKS):
        at = slice(b * step, (b + 1) * step)
        out_ref[at, :] = sum_ref[at, :] + from_i16(got_ref[at, :]) * scale[b : b + 1]


def quantize(values_a, values_b):
    code_a = code_of(jnp.max(jnp.abs(values_a), axis=1, keepdims=True))
    code_b = code_of(jnp.max(jnp.abs(values_b), axis=1, keepdims=True))
    lane = lax.broadcasted_iota(I32, (values_a.shape[0], 128), 1)
    codes = jnp.where(lane == 0, code_a, code_b)
    inverse = TOP / scale_of(codes)
    q_a = to_i16(values_a * inverse[:, 0:1])
    q_b = to_i16(values_b * inverse[:, 1:2])
    return q_a, q_b, codes


def grad_kernel(
    owner_ref, mine_ref, other_ref, acts_ref, cot_ref, out_ref, full_ref, low_ref, left_ref, fa_ref, fb_ref
):
    tokens, wide_a = acts_ref.shape
    wide_b = cot_ref.shape[1]
    half = tokens // 2
    core = lax.rem(lax.axis_index("mp"), 2)
    full_ref[pl.ds(pl.multiple_of(core * half, half), half), :] = mine_ref[...]
    full_ref[pl.ds(pl.multiple_of((1 - core) * half, half), half), :] = other_ref[...]
    low = full_ref[...].T
    high = low.astype(BF16).astype(F32)
    low_ref[0] = high
    low_ref[1] = low - high
    mask = owner_ref[...] == lax.broadcasted_iota(I32, (POLICIES, tokens), 0)

    def spread(side, first_rank):
        for part in range(2):
            for k in range(4):
                for d in range(4):
                    start = first_rank + jnp.where(core == 0, k * 16 + d * 4, d * 16 + k * 4)
                    at = part * 256 + (k % 2) * 128 + d * 32
                    rows = []
                    for i in range(4):
                        row = low_ref[part, pl.ds(start + i, 1), :]
                        rows.append(jnp.where(mask, jnp.broadcast_to(row, mask.shape), 0.0))
                    left_ref[side, k // 2, at : at + 32, :] = jnp.concatenate(rows, axis=0).astype(BF16)

    spread(0, RANK)
    spread(1, 0)
    quarter = full_rows(out_ref, wide_a + wide_b)
    for h in range(2):
        rows = slice(h * 2 * quarter, (h + 1) * 2 * quarter)
        for side, x_ref, f_ref in ((0, acts_ref, fa_ref), (1, cot_ref, fb_ref)):
            left = left_ref[side, h]
            width = x_ref.shape[1]
            for c0 in range(0, width, 256):
                c1 = min(c0 + 256, width)
                both = jnp.dot(left, x_ref[:, c0:c1], preferred_element_type=F32)
                f_ref[rows, c0:c1] = both[: 2 * quarter] + both[2 * quarter :]
        for k in (2 * h, 2 * h + 1):
            at = slice(k * quarter, (k + 1) * quarter)
            q_a, q_b, codes = quantize(fa_ref[at, :], fb_ref[at, :])
            store_columns(out_ref, k, q_a, q_b)
            out_ref[k, -16:, :] = codes.T[:16].astype(I32).astype(I16)


def full_rows(ref, width):
    return (ref.shape[1] - 16) // (width // 128)


def store_columns(out_ref, k, q_a, q_b):
    rows, at = q_a.shape[0], 0
    for q in (q_a, q_b):
        for c in range(0, q.shape[1], 128):
            out_ref[k, at : at + rows, :] = q[:, c : c + 128]
            at += rows


def sum_parts(scales, parts):
    total_a = total_b = None
    for (s_a, s_b), (a, b) in zip(scales, parts):
        a, b = from_i16(a) * s_a, from_i16(b) * s_b
        total_a = a if total_a is None else total_a + a
        total_b = b if total_b is None else total_b + b
    return total_a, total_b


def second_kernel(wide_a, wide_b, got_ref, out_ref):
    rows = full_rows(got_ref, wide_a + wide_b)
    n_a, n_b = wide_a // 128, wide_b // 128
    scales = []
    for k in range(4):
        codes = from_i16(got_ref[k, -16:, :])
        codes = scale_of(jnp.concatenate([codes, jnp.zeros((112, 128), F32)], axis=0).T) * (1.0 / TOP)
        scales.append((codes[:, 0:1], codes[:, 1:2]))

    def column(c):
        total = None
        for k in range(4):
            part = from_i16(got_ref[k, c * rows : (c + 1) * rows, :]) * scales[k][0 if c < n_a else 1]
            total = part if total is None else total + part
        return total

    total_a = jnp.concatenate([column(c) for c in range(n_a)], axis=1)
    total_b = jnp.concatenate([column(c) for c in range(n_a, n_a + n_b)], axis=1)
    q_a, q_b, codes = quantize(total_a, total_b)
    codes = codes.astype(I32).astype(I16)
    rows = out_ref.shape[1]
    for k in range(4):
        at = slice(k * rows, (k + 1) * rows)
        out_ref[k, :, :wide_a] = q_a[at]
        out_ref[k, :, wide_a : wide_a + wide_b] = q_b[at]
        out_ref[k, :, wide_a + wide_b :] = codes[at]


def third_kernel(wide_a, wide_b, got_ref, out_ref, total_ref):
    parts, scales = [], []
    for k in range(4):
        codes = scale_of(from_i16(got_ref[k, :, wide_a + wide_b :])) * (1.0 / TOP)
        scales.append((codes[:, 0:1], codes[:, 1:2]))
        parts.append((got_ref[k, :, :wide_a], got_ref[k, :, wide_a : wide_a + wide_b]))
    total_a, total_b = sum_parts(scales, parts)
    n_a, n_b = wide_a // 128, wide_b // 128
    for c in range(n_a):
        total_ref[c * 32 : (c + 1) * 32, :] = total_a[:, c * 128 : (c + 1) * 128]
    for c in range(n_b):
        total_ref[(n_a + c) * 32 : (n_a + c + 1) * 32, :] = total_b[:, c * 128 : (c + 1) * 128]

    def code_for(parts):
        most = jnp.abs(parts[0])
        for part in parts[1:]:
            most = jnp.maximum(most, jnp.abs(part))
        return code_of(jnp.max(jnp.max(most, axis=0, keepdims=True), axis=1, keepdims=True))

    def piece_of(p):
        parts = [total_ref[pl.ds(c * 32 + p, 4, stride=POLICIES), :] for c in range(n_a + n_b)]
        code_a, code_b = code_for(parts[:n_a]), code_for(parts[n_a:])
        pieces = [part * (TOP / scale_of(code_a)) for part in parts[:n_a]]
        pieces += [part * (TOP / scale_of(code_b)) for part in parts[n_a:]]
        row = lax.broadcasted_iota(I32, (4, 128), 0)
        return pieces + [jnp.where(row == 0, code_a, code_b)]

    for m in range(NEAR):
        pieces = []
        for p in range(m, POLICIES, NEAR):
            pieces += piece_of(p)
        out_ref[m] = to_i16(jnp.concatenate(pieces, axis=0))


def open_piece(values, n_a, n_b):
    at = 4 * (n_a + n_b)
    s_a = scale_of(values[at : at + 1]) * (1.0 / TOP)
    s_b = scale_of(values[at + 1 : at + 2]) * (1.0 / TOP)
    row = lax.broadcasted_iota(I32, values.shape, 0)
    return values * jnp.where(row < 4 * n_a, s_a, s_b)


def fourth_kernel(wide_a, wide_b, got_ref, mine_ref, out_ref):
    n_a, n_b = wide_a // 128, wide_b // 128
    deep = 4 * (n_a + n_b) + 4
    low = high = None
    for k in range(NEAR):
        values = from_i16(got_ref[k])
        first, second = open_piece(values[:deep], n_a, n_b), open_piece(values[deep:], n_a, n_b)
        low = first if low is None else low + first
        high = second if high is None else high + second
    upper = lax.axis_index("dp") // 16 >= NEAR
    mine_ref[...] = jnp.where(upper, high, low)
    other = jnp.where(upper, low, high)
    row = lax.broadcasted_iota(I32, other.shape, 0)

    def code_for(first, last):
        most = jnp.where((row >= first) & (row < last), jnp.abs(other), 0.0)
        return code_of(jnp.max(jnp.max(most, axis=0, keepdims=True), axis=1, keepdims=True))

    code_a, code_b = code_for(0, 4 * n_a), code_for(4 * n_a, deep - 4)
    values = other * jnp.where(row < 4 * n_a, TOP / scale_of(code_a), TOP / scale_of(code_b))
    values = jnp.where(row < deep - 4, values, jnp.where(row == deep - 4, code_a, code_b))
    out_ref[...] = to_i16(jnp.concatenate([values, jnp.zeros((8, 128), F32)], axis=0))


def last_kernel(wide_a, wide_b, mine_ref, got_ref, a_ref, b_ref):
    n_a, n_b = wide_a // 128, wide_b // 128
    values = from_i16(got_ref[...])[: mine_ref.shape[0]]
    total = mine_ref[...] + open_piece(values, n_a, n_b)
    for c in range(n_a):
        a_ref[:, c * 128 : (c + 1) * 128] = total[c * 4 : (c + 1) * 4]
    for c in range(n_b):
        b_ref[:, c * 128 : (c + 1) * 128] = total[4 * (n_a + c) : 4 * (n_a + c + 1)]


def call(kernel, outs, spaces, scratch=()):
    return pl.pallas_call(
        kernel,
        out_shape=[jax.ShapeDtypeStruct(s, d) for s, d in outs],
        in_specs=[pl.BlockSpec(memory_space=m) for m in spaces],
        out_specs=[pl.BlockSpec(memory_space=pltpu.VMEM)] * len(outs),
        scratch_shapes=list(scratch),
        compiler_params=pltpu.CompilerParams(vmem_limit_bytes=40 * 1024 * 1024),
    )


def in_hbm(array):
    return pltpu.with_memory_space_constraint(array, pltpu.HBM)


def groups_of():
    index = np.arange(512).reshape(8, 4, 4, 2, 2)
    first, second = [], []
    for z in range(8):
        for h in range(2):
            for k in range(4):
                first.append(index[z, :, k, h, 0].tolist())
                first.append(index[z, k, :, h, 1].tolist())
                second.append(index[z, k, :, h, 0].tolist())
                second.append(index[z, :, k, h, 1].tolist())
    third = [
        index[z : z + NEAR, x, y, h, c].tolist()
        for z in (0, NEAR)
        for x in range(4)
        for y in range(4)
        for h in range(2)
        for c in range(2)
    ]
    return first, second, third


def shards(acts, cot, lengths, policy, advantages, old, new, down, up):
    tokens, wide_a = acts.shape
    wide_b = cot.shape[1]
    half = tokens // 2
    first, second, third = groups_of()
    core_pairs = [(0, 1), (1, 0), (2, 3), (3, 2)]
    far_pairs = [(0, 2), (2, 0), (1, 3), (3, 1)]
    lines = (tokens // 128, 128)
    keep, send, owner, acts, cot = call(
        low_kernel,
        [((half, 128), F32)] * 2 + [((POLICIES, tokens), I32), (acts.shape, BF16), (cot.shape, BF16)],
        [HBM] * 9,
        [
            VMEM((tokens, 128), F32),
            SMEM(lengths.shape, I32),
            SMEM(policy.shape, I32),
            SMEM(advantages.shape, F32),
            VMEM(lines, F32),
            VMEM(lines, F32),
            VMEM(down.shape, BF16),
            VMEM(up.shape, BF16),
            pltpu.SemaphoreType.DMA((11,)),
        ],
    )(*map(in_hbm, (lengths, policy, advantages, old.reshape(lines), new.reshape(lines), acts, cot, down, up)))
    got = lax.ppermute(send, "mp", core_pairs)
    part, packed = call(pack_kernel, [((half, 128), F32), ((half + 16, 128), I16)], [VMEM] * 2)(keep, got)
    far = lax.ppermute(packed, "mp", far_pairs)
    (mine,) = call(unpack_kernel, [((half, 128), F32)], [VMEM] * 2)(part, far)
    other = lax.ppermute(mine, "mp", core_pairs)
    rows = POLICIES * RANK
    width = wide_a + wide_b + 128
    (pieces,) = call(
        grad_kernel,
        [((4, rows // 4 * (wide_a + wide_b) // 128 + 16, 128), I16)],
        [VMEM] * 5,
        [
            VMEM((tokens, 128), F32),
            VMEM((2, 2 * RANK, tokens), F32),
            VMEM((2, 2, rows, tokens), BF16),
            VMEM((rows, wide_a), F32),
            VMEM((rows, wide_b), F32),
        ],
    )(owner, mine, other, acts, cot)
    got = lax.all_to_all(pieces, BOTH, 0, 0, tiled=True, axis_index_groups=first)
    (pieces,) = call(
        functools.partial(second_kernel, wide_a, wide_b), [((4, rows // 16, width), I16)], [VMEM]
    )(got)
    got = lax.all_to_all(pieces, BOTH, 0, 0, tiled=True, axis_index_groups=second)
    deep = 4 * (wide_a + wide_b) // 128 + 4
    (pieces,) = call(
        functools.partial(third_kernel, wide_a, wide_b), [((NEAR, 2 * deep, 128), I16)], [VMEM], [VMEM((rows // 16 * (wide_a + wide_b) // 128, 128), F32)]
    )(got)
    got = lax.all_to_all(pieces, BOTH, 0, 0, tiled=True, axis_index_groups=third)
    part, packed = call(
        functools.partial(fourth_kernel, wide_a, wide_b),
        [((deep, 128), F32), ((deep + 8, 128), I16)],
        [VMEM],
    )(got)
    count = lax.axis_size("dp")
    got = lax.ppermute(packed, "dp", [(i, (i + count // 2) % count) for i in range(count)])
    return tuple(
        call(
            functools.partial(last_kernel, wide_a, wide_b), [((4, wide_a), F32), ((4, wide_b), F32)], [VMEM] * 2
        )(part, got)
    )


def solution(mesh):
    return jax.shard_map(
        shards,
        mesh=mesh,
        in_specs=(
            P("dp", "mp"),
            P("dp", "mp"),
            P("dp", None),
            P("dp", None),
            P("dp", None),
            P("dp"),
            P("dp"),
            P("mp", None),
            P(None, "mp"),
        ),
        out_specs=(P("dp", "mp"), P("dp", "mp")),
        check_vma=False,
    )
```

```python
import functools

import jax
import jax.numpy as jnp
import numpy as np
from jax import lax
from jax.experimental import pallas as pl
from jax.experimental.pallas import tpu as pltpu
from jax.sharding import PartitionSpec as P

RANK = 64
POLICIES = 8
SEQS = 8
ADAPTER_SCALE = 2.0
CLIP_LOW = 0.8
CLIP_HIGH = 1.28
TINY = 1e-30
TOP = 32767.0
F32, BF16, I16, I32 = jnp.float32, jnp.bfloat16, jnp.int16, jnp.int32
BOTH = ("dp", "mp")
VMEM, SMEM, HBM = pltpu.VMEM, pltpu.SMEM, pltpu.HBM


def code_of(largest):
    return jnp.ceil(jnp.log2(jnp.maximum(largest, TINY)) * 256.0) + 1.0


def scale_of(code):
    return jnp.exp2(code * (1.0 / 256.0))


def to_i16(values):
    return jnp.round(values).astype(I32).astype(I16)


def from_i16(values):
    return values.astype(I32).astype(F32)


def starts_of(lengths_ref):
    bounds = [jnp.int32(0)]
    for s in range(SEQS):
        bounds.append(bounds[-1] + lengths_ref[0, s])
    return bounds


CUT = 512


def low_kernel(
    lengths_hbm, policy_hbm, adv_hbm, old_hbm, new_hbm, acts_hbm, cot_hbm, down_hbm, up_hbm,
    keep_ref, send_ref, owner_ref, acts_ref, cot_ref,
    x_ref, lengths_ref, policy_ref, adv_ref, old_ref, new_ref, down_ref, up_ref, sems,
):
    tokens, wide_a = acts_ref.shape
    half = tokens // 2
    pairs = [
        (lengths_hbm, lengths_ref),
        (policy_hbm, policy_ref),
        (adv_hbm, adv_ref),
        (old_hbm, old_ref),
        (new_hbm, new_ref),
        (cot_hbm, cot_ref),
        (up_hbm, up_ref),
        (acts_hbm.at[:, :CUT], acts_ref.at[:, :CUT]),
        (down_hbm.at[:CUT, :], down_ref.at[:CUT, :]),
        (acts_hbm.at[:, CUT:], acts_ref.at[:, CUT:]),
        (down_hbm.at[CUT:, :], down_ref.at[CUT:, :]),
    ]
    copies = [pltpu.make_async_copy(src, dst, sems.at[i]) for i, (src, dst) in enumerate(pairs)]
    for copy in copies:
        copy.start()
    for copy in copies[:5]:
        copy.wait()
    bounds = starts_of(lengths_ref)
    row = lax.broadcasted_iota(I32, (tokens, 128), 0)
    lane = lax.broadcasted_iota(I32, (tokens, 128), 1)
    owner = jnp.full((tokens, 128), -1, I32)
    factor = jnp.zeros((tokens, 128), F32)
    for s in range(SEQS):
        inside = (row >= bounds[s]) & (row < bounds[s + 1])
        total = jnp.full((8, 128), adv_ref[0, s], F32) / jnp.full((8, 128), lengths_ref[0, s], I32).astype(F32)
        owner = jnp.where(inside, policy_ref[0, s], owner)
        factor = jnp.where(inside, total[0:1, :], factor)
    pos = lax.broadcasted_iota(I32, (POLICIES, tokens), 1)
    held = jnp.full((POLICIES, tokens), -1, I32)
    for s in range(SEQS):
        held = jnp.where((pos >= bounds[s]) & (pos < bounds[s + 1]), policy_ref[0, s], held)
    owner_ref[...] = held
    ratio = jnp.clip(jnp.exp(new_ref[...] - old_ref[...]), CLIP_LOW, CLIP_HIGH) * ADAPTER_SCALE
    groups = ratio.shape[0]
    ratio = jnp.concatenate([ratio, jnp.zeros((128 - groups, 128), F32)], axis=0).T
    ratio = jnp.concatenate([ratio[:, j : j + 1] for j in range(groups)], axis=0)
    weight = factor * ratio

    def own(full):
        total = jnp.zeros((tokens, 128), F32)
        for j in range(POLICIES // 2):
            mine = owner == 2 * j + jnp.where(lane >= RANK, 1, 0)
            total = total + jnp.where(mine, full[:, j * 128 : (j + 1) * 128], 0.0)
        return total + pltpu.roll(total, RANK, 1)

    copies[5].wait()
    copies[6].wait()
    low_out = own(
        lax.dot_general(cot_ref[...], up_ref[...], (((1,), (1,)), ((), ())), preferred_element_type=F32)
    )
    copies[7].wait()
    copies[8].wait()
    low_in = jnp.dot(acts_ref[:, :CUT], down_ref[:CUT, :], preferred_element_type=F32)
    copies[9].wait()
    copies[10].wait()
    low_in = own(low_in + jnp.dot(acts_ref[:, CUT:], down_ref[CUT:, :], preferred_element_type=F32))
    x_ref[...] = jnp.where(lane < RANK, low_in, low_out) * weight
    core = lax.rem(lax.axis_index("mp"), 2)
    keep_ref[...] = x_ref[pl.ds(pl.multiple_of(core * half, half), half), :]
    send_ref[...] = x_ref[pl.ds(pl.multiple_of((1 - core) * half, half), half), :]


BLOCKS = 4
NEAR = 4


def pack_kernel(keep_ref, got_ref, sum_ref, out_ref):
    half = keep_ref.shape[0]
    step = half // BLOCKS
    total = keep_ref[...] + got_ref[...]
    sum_ref[...] = total
    codes = []
    for b in range(BLOCKS):
        part = total[b * step : (b + 1) * step]
        code = code_of(jnp.max(jnp.abs(part), axis=0, keepdims=True))
        codes.append(code)
        out_ref[b * step : (b + 1) * step, :] = to_i16(part * (TOP / scale_of(code)))
    codes.append(jnp.zeros((16 - BLOCKS, 128), F32))
    out_ref[half:, :] = jnp.concatenate(codes, axis=0).astype(I32).astype(I16)


def unpack_kernel(sum_ref, got_ref, out_ref):
    half = sum_ref.shape[0]
    step = half // BLOCKS
    scale = scale_of(from_i16(got_ref[half:, :])) * (1.0 / TOP)
    for b in range(BLOCKS):
        at = slice(b * step, (b + 1) * step)
        out_ref[at, :] = sum_ref[at, :] + from_i16(got_ref[at, :]) * scale[b : b + 1]


def quantize(values_a, values_b):
    code_a = code_of(jnp.max(jnp.abs(values_a), axis=1, keepdims=True))
    code_b = code_of(jnp.max(jnp.abs(values_b), axis=1, keepdims=True))
    lane = lax.broadcasted_iota(I32, (values_a.shape[0], 128), 1)
    codes = jnp.where(lane == 0, code_a, code_b)
    inverse = TOP / scale_of(codes)
    q_a = to_i16(values_a * inverse[:, 0:1])
    q_b = to_i16(values_b * inverse[:, 1:2])
    return q_a, q_b, codes


def half_gradients(other, owner_ref, half_ref, acts_ref, cot_ref, low_ref, left_ref, store):
    half = half_ref.shape[0]
    core = lax.rem(lax.axis_index("mp"), 2)
    tokens = pl.ds(pl.multiple_of((1 - core if other else core) * half, half), half)
    low = half_ref[...].T
    high = low.astype(BF16).astype(F32)
    low_ref[0] = high
    low_ref[1] = low - high
    mask = owner_ref[:, tokens] == lax.broadcasted_iota(I32, (POLICIES, half), 0)
    for side, first_rank in ((0, RANK), (1, 0)):
        for part in range(2):
            for k in range(4):
                for d in range(4):
                    start = first_rank + jnp.where(core == 0, k * 16 + d * 4, d * 16 + k * 4)
                    at = part * 256 + (k % 2) * 128 + d * 32
                    rows = []
                    for i in range(4):
                        row = low_ref[part, pl.ds(start + i, 1), :]
                        rows.append(jnp.where(mask, jnp.broadcast_to(row, mask.shape), 0.0))
                    left_ref[side, k // 2, at : at + 32, :] = jnp.concatenate(rows, axis=0).astype(BF16)
    for h in range(2):
        rows, at = slice(h * 256, (h + 1) * 256), 0
        for side, x_ref in ((0, acts_ref), (1, cot_ref)):
            left = left_ref[side, h]
            width = x_ref.shape[1]
            for c0 in range(0, width, 256):
                c1 = min(c0 + 256, width)
                both = jnp.dot(left, x_ref[tokens, c0:c1], preferred_element_type=F32)
                store(rows, slice(at + c0, at + c1), both[:256] + both[256:])
            at += width
        yield h


def own_kernel(owner_ref, half_ref, acts_ref, cot_ref, sum_ref, low_ref, left_ref):
    def store(rows, columns, values):
        sum_ref[rows, columns] = values

    for _ in half_gradients(False, owner_ref, half_ref, acts_ref, cot_ref, low_ref, left_ref, store):
        pass


def grad_kernel(owner_ref, half_ref, acts_ref, cot_ref, sum_ref, out_ref, low_ref, left_ref, f_ref):
    wide_a, wide_b = acts_ref.shape[1], cot_ref.shape[1]
    quarter = full_rows(out_ref, wide_a + wide_b)

    def store(rows, columns, values):
        f_ref[rows, columns] = values + sum_ref[rows, columns]

    for h in half_gradients(True, owner_ref, half_ref, acts_ref, cot_ref, low_ref, left_ref, store):
        for k in (2 * h, 2 * h + 1):
            at = slice(k * quarter, (k + 1) * quarter)
            q_a, q_b, codes = quantize(f_ref[at, :wide_a], f_ref[at, wide_a:])
            store_columns(out_ref, k, q_a, q_b)
            out_ref[k, -16:, :] = codes.T[:16].astype(I32).astype(I16)


def full_rows(ref, width):
    return (ref.shape[1] - 16) // (width // 128)


def store_columns(out_ref, k, q_a, q_b):
    rows, at = q_a.shape[0], 0
    for q in (q_a, q_b):
        for c in range(0, q.shape[1], 128):
            out_ref[k, at : at + rows, :] = q[:, c : c + 128]
            at += rows


def sum_parts(scales, parts):
    total_a = total_b = None
    for (s_a, s_b), (a, b) in zip(scales, parts):
        a, b = from_i16(a) * s_a, from_i16(b) * s_b
        total_a = a if total_a is None else total_a + a
        total_b = b if total_b is None else total_b + b
    return total_a, total_b


def second_kernel(wide_a, wide_b, got_ref, out_ref):
    rows = full_rows(got_ref, wide_a + wide_b)
    n_a, n_b = wide_a // 128, wide_b // 128
    scales = []
    for k in range(4):
        codes = from_i16(got_ref[k, -16:, :])
        codes = scale_of(jnp.concatenate([codes, jnp.zeros((112, 128), F32)], axis=0).T) * (1.0 / TOP)
        scales.append((codes[:, 0:1], codes[:, 1:2]))

    def column(c):
        total = None
        for k in range(4):
            part = from_i16(got_ref[k, c * rows : (c + 1) * rows, :]) * scales[k][0 if c < n_a else 1]
            total = part if total is None else total + part
        return total

    total_a = jnp.concatenate([column(c) for c in range(n_a)], axis=1)
    total_b = jnp.concatenate([column(c) for c in range(n_a, n_a + n_b)], axis=1)
    q_a, q_b, codes = quantize(total_a, total_b)
    codes = codes.astype(I32).astype(I16)
    rows = out_ref.shape[1]
    for k in range(4):
        at = slice(k * rows, (k + 1) * rows)
        out_ref[k, :, :wide_a] = q_a[at]
        out_ref[k, :, wide_a : wide_a + wide_b] = q_b[at]
        out_ref[k, :, wide_a + wide_b :] = codes[at]


def third_kernel(wide_a, wide_b, got_ref, out_ref, total_ref):
    parts, scales = [], []
    for k in range(4):
        codes = scale_of(from_i16(got_ref[k, :, wide_a + wide_b :])) * (1.0 / TOP)
        scales.append((codes[:, 0:1], codes[:, 1:2]))
        parts.append((got_ref[k, :, :wide_a], got_ref[k, :, wide_a : wide_a + wide_b]))
    total_a, total_b = sum_parts(scales, parts)
    n_a, n_b = wide_a // 128, wide_b // 128
    for c in range(n_a):
        total_ref[c * 32 : (c + 1) * 32, :] = total_a[:, c * 128 : (c + 1) * 128]
    for c in range(n_b):
        total_ref[(n_a + c) * 32 : (n_a + c + 1) * 32, :] = total_b[:, c * 128 : (c + 1) * 128]

    def code_for(parts):
        most = jnp.abs(parts[0])
        for part in parts[1:]:
            most = jnp.maximum(most, jnp.abs(part))
        return code_of(jnp.max(jnp.max(most, axis=0, keepdims=True), axis=1, keepdims=True))

    def piece_of(p):
        parts = [total_ref[pl.ds(c * 32 + p, 4, stride=POLICIES), :] for c in range(n_a + n_b)]
        code_a, code_b = code_for(parts[:n_a]), code_for(parts[n_a:])
        pieces = [part * (TOP / scale_of(code_a)) for part in parts[:n_a]]
        pieces += [part * (TOP / scale_of(code_b)) for part in parts[n_a:]]
        row = lax.broadcasted_iota(I32, (4, 128), 0)
        return pieces + [jnp.where(row == 0, code_a, code_b)]

    for m in range(NEAR):
        pieces = []
        for p in range(m, POLICIES, NEAR):
            pieces += piece_of(p)
        out_ref[m] = to_i16(jnp.concatenate(pieces, axis=0))


def open_piece(values, n_a, n_b):
    at = 4 * (n_a + n_b)
    s_a = scale_of(values[at : at + 1]) * (1.0 / TOP)
    s_b = scale_of(values[at + 1 : at + 2]) * (1.0 / TOP)
    row = lax.broadcasted_iota(I32, values.shape, 0)
    return values * jnp.where(row < 4 * n_a, s_a, s_b)


def fourth_kernel(wide_a, wide_b, got_ref, mine_ref, out_ref):
    n_a, n_b = wide_a // 128, wide_b // 128
    deep = 4 * (n_a + n_b) + 4
    low = high = None
    for k in range(NEAR):
        values = from_i16(got_ref[k])
        first, second = open_piece(values[:deep], n_a, n_b), open_piece(values[deep:], n_a, n_b)
        low = first if low is None else low + first
        high = second if high is None else high + second
    upper = lax.axis_index("dp") // 16 >= NEAR
    mine_ref[...] = jnp.where(upper, high, low)
    other = jnp.where(upper, low, high)
    row = lax.broadcasted_iota(I32, other.shape, 0)

    def code_for(first, last):
        most = jnp.where((row >= first) & (row < last), jnp.abs(other), 0.0)
        return code_of(jnp.max(jnp.max(most, axis=0, keepdims=True), axis=1, keepdims=True))

    code_a, code_b = code_for(0, 4 * n_a), code_for(4 * n_a, deep - 4)
    values = other * jnp.where(row < 4 * n_a, TOP / scale_of(code_a), TOP / scale_of(code_b))
    values = jnp.where(row < deep - 4, values, jnp.where(row == deep - 4, code_a, code_b))
    out_ref[...] = to_i16(jnp.concatenate([values, jnp.zeros((8, 128), F32)], axis=0))


def last_kernel(wide_a, wide_b, mine_ref, got_ref, a_ref, b_ref):
    n_a, n_b = wide_a // 128, wide_b // 128
    values = from_i16(got_ref[...])[: mine_ref.shape[0]]
    total = mine_ref[...] + open_piece(values, n_a, n_b)
    for c in range(n_a):
        a_ref[:, c * 128 : (c + 1) * 128] = total[c * 4 : (c + 1) * 4]
    for c in range(n_b):
        b_ref[:, c * 128 : (c + 1) * 128] = total[4 * (n_a + c) : 4 * (n_a + c + 1)]


def call(kernel, outs, spaces, scratch=()):
    return pl.pallas_call(
        kernel,
        out_shape=[jax.ShapeDtypeStruct(s, d) for s, d in outs],
        in_specs=[pl.BlockSpec(memory_space=m) for m in spaces],
        out_specs=[pl.BlockSpec(memory_space=pltpu.VMEM)] * len(outs),
        scratch_shapes=list(scratch),
        compiler_params=pltpu.CompilerParams(vmem_limit_bytes=40 * 1024 * 1024),
    )


def in_hbm(array):
    return pltpu.with_memory_space_constraint(array, pltpu.HBM)


def groups_of():
    index = np.arange(512).reshape(8, 4, 4, 2, 2)
    first, second = [], []
    for z in range(8):
        for h in range(2):
            for k in range(4):
                first.append(index[z, :, k, h, 0].tolist())
                first.append(index[z, k, :, h, 1].tolist())
                second.append(index[z, k, :, h, 0].tolist())
                second.append(index[z, :, k, h, 1].tolist())
    third = [
        index[z : z + NEAR, x, y, h, c].tolist()
        for z in (0, NEAR)
        for x in range(4)
        for y in range(4)
        for h in range(2)
        for c in range(2)
    ]
    return first, second, third


def shards(acts, cot, lengths, policy, advantages, old, new, down, up):
    tokens, wide_a = acts.shape
    wide_b = cot.shape[1]
    half = tokens // 2
    first, second, third = groups_of()
    core_pairs = [(0, 1), (1, 0), (2, 3), (3, 2)]
    far_pairs = [(0, 2), (2, 0), (1, 3), (3, 1)]
    lines = (tokens // 128, 128)
    keep, send, owner, acts, cot = call(
        low_kernel,
        [((half, 128), F32)] * 2 + [((POLICIES, tokens), I32), (acts.shape, BF16), (cot.shape, BF16)],
        [HBM] * 9,
        [
            VMEM((tokens, 128), F32),
            SMEM(lengths.shape, I32),
            SMEM(policy.shape, I32),
            SMEM(advantages.shape, F32),
            VMEM(lines, F32),
            VMEM(lines, F32),
            VMEM(down.shape, BF16),
            VMEM(up.shape, BF16),
            pltpu.SemaphoreType.DMA((11,)),
        ],
    )(*map(in_hbm, (lengths, policy, advantages, old.reshape(lines), new.reshape(lines), acts, cot, down, up)))
    got = lax.ppermute(send, "mp", core_pairs)
    part, packed = call(pack_kernel, [((half, 128), F32), ((half + 16, 128), I16)], [VMEM] * 2)(keep, got)
    far = lax.ppermute(packed, "mp", far_pairs)
    (mine,) = call(unpack_kernel, [((half, 128), F32)], [VMEM] * 2)(part, far)
    other = lax.ppermute(mine, "mp", core_pairs)
    rows = POLICIES * RANK
    width = wide_a + wide_b + 128
    scratch = [VMEM((2, 2 * RANK, half), F32), VMEM((2, 2, rows, half), BF16)]
    total = ((rows, wide_a + wide_b), F32)
    (own,) = call(own_kernel, [total], [VMEM] * 4, scratch)(owner, mine, acts, cot)
    (pieces,) = call(
        grad_kernel,
        [((4, rows // 4 * (wide_a + wide_b) // 128 + 16, 128), I16)],
        [VMEM] * 5,
        scratch + [VMEM(*total)],
    )(owner, other, acts, cot, own)
    got = lax.all_to_all(pieces, BOTH, 0, 0, tiled=True, axis_index_groups=first)
    (pieces,) = call(
        functools.partial(second_kernel, wide_a, wide_b), [((4, rows // 16, width), I16)], [VMEM]
    )(got)
    got = lax.all_to_all(pieces, BOTH, 0, 0, tiled=True, axis_index_groups=second)
    deep = 4 * (wide_a + wide_b) // 128 + 4
    (pieces,) = call(
        functools.partial(third_kernel, wide_a, wide_b), [((NEAR, 2 * deep, 128), I16)], [VMEM], [VMEM((rows // 16 * (wide_a + wide_b) // 128, 128), F32)]
    )(got)
    got = lax.all_to_all(pieces, BOTH, 0, 0, tiled=True, axis_index_groups=third)
    part, packed = call(
        functools.partial(fourth_kernel, wide_a, wide_b),
        [((deep, 128), F32), ((deep + 8, 128), I16)],
        [VMEM],
    )(got)
    count = lax.axis_size("dp")
    got = lax.ppermute(packed, "dp", [(i, (i + count // 2) % count) for i in range(count)])
    return tuple(
        call(
            functools.partial(last_kernel, wide_a, wide_b), [((4, wide_a), F32), ((4, wide_b), F32)], [VMEM] * 2
        )(part, got)
    )


def solution(mesh):
    return jax.shard_map(
        shards,
        mesh=mesh,
        in_specs=(
            P("dp", "mp"),
            P("dp", "mp"),
            P("dp", None),
            P("dp", None),
            P("dp", None),
            P("dp"),
            P("dp"),
            P("mp", None),
            P(None, "mp"),
        ),
        out_specs=(P("dp", "mp"), P("dp", "mp")),
        check_vma=False,
    )
```

```python
import functools

import jax
import jax.numpy as jnp
import numpy as np
from jax import lax
from jax.experimental import pallas as pl
from jax.experimental.pallas import tpu as pltpu
from jax.sharding import PartitionSpec as P

RANK = 64
POLICIES = 8
SEQS = 8
ADAPTER_SCALE = 2.0
CLIP_LOW = 0.8
CLIP_HIGH = 1.28
TINY = 1e-30
TOP = 32767.0
F32, BF16, I16, I32 = jnp.float32, jnp.bfloat16, jnp.int16, jnp.int32
BOTH = ("dp", "mp")
VMEM, SMEM, HBM = pltpu.VMEM, pltpu.SMEM, pltpu.HBM


def code_of(largest):
    return jnp.ceil(jnp.log2(jnp.maximum(largest, TINY)) * 256.0) + 1.0


def scale_of(code):
    return jnp.exp2(code * (1.0 / 256.0))


def to_i16(values):
    return jnp.round(values).astype(I32).astype(I16)


def from_i16(values):
    return values.astype(I32).astype(F32)


def starts_of(lengths_ref):
    bounds = [jnp.int32(0)]
    for s in range(SEQS):
        bounds.append(bounds[-1] + lengths_ref[0, s])
    return bounds


CUT = 512


def low_kernel(
    lengths_hbm, policy_hbm, adv_hbm, old_hbm, new_hbm, acts_hbm, cot_hbm, down_hbm, up_hbm,
    send_ref, owner_ref, acts_ref, cot_ref, down_ref, up_ref, member_ref, weight_ref,
    lengths_ref, policy_ref, adv_ref, old_ref, new_ref, sems,
):
    tokens, wide_a = acts_ref.shape
    pairs = [
        (lengths_hbm, lengths_ref),
        (policy_hbm, policy_ref),
        (adv_hbm, adv_ref),
        (old_hbm, old_ref),
        (new_hbm, new_ref),
        (cot_hbm, cot_ref),
        (up_hbm, up_ref),
        (acts_hbm.at[:, :CUT], acts_ref.at[:, :CUT]),
        (down_hbm.at[:CUT, :], down_ref.at[:CUT, :]),
        (acts_hbm.at[:, CUT:], acts_ref.at[:, CUT:]),
        (down_hbm.at[CUT:, :], down_ref.at[CUT:, :]),
    ]
    copies = [pltpu.make_async_copy(src, dst, sems.at[i]) for i, (src, dst) in enumerate(pairs)]
    for copy in copies:
        copy.start()
    for copy in copies[:5]:
        copy.wait()
    bounds = starts_of(lengths_ref)
    row = lax.broadcasted_iota(I32, (tokens, 128), 0)
    lane = lax.broadcasted_iota(I32, (tokens, 128), 1)
    owner = jnp.full((tokens, 128), -1, I32)
    factor = jnp.zeros((tokens, 128), F32)
    for s in range(SEQS):
        inside = (row >= bounds[s]) & (row < bounds[s + 1])
        total = jnp.full((8, 128), adv_ref[0, s], F32) / jnp.full((8, 128), lengths_ref[0, s], I32).astype(F32)
        owner = jnp.where(inside, policy_ref[0, s], owner)
        factor = jnp.where(inside, total[0:1, :], factor)
    pos = lax.broadcasted_iota(I32, (POLICIES, tokens), 1)
    held = jnp.full((POLICIES, tokens), -1, I32)
    for s in range(SEQS):
        held = jnp.where((pos >= bounds[s]) & (pos < bounds[s + 1]), policy_ref[0, s], held)
    owner_ref[...] = held
    ratio = jnp.clip(jnp.exp(new_ref[...] - old_ref[...]), CLIP_LOW, CLIP_HIGH) * ADAPTER_SCALE
    groups = ratio.shape[0]
    ratio = jnp.concatenate([ratio, jnp.zeros((128 - groups, 128), F32)], axis=0).T
    ratio = jnp.concatenate([ratio[:, j : j + 1] for j in range(groups)], axis=0)
    weight_ref[...] = factor * ratio
    member_ref[...] = owner

    def wait(group):
        for copy in copies[group]:
            copy.wait()

    half_products(True, acts_ref, cot_ref, down_ref, up_ref, member_ref, weight_ref, send_ref, wait)


def half_products(other, acts_ref, cot_ref, down_ref, up_ref, member_ref, weight_ref, out_ref, wait):
    half = out_ref.shape[0]
    core = lax.rem(lax.axis_index("mp"), 2)
    tokens = pl.ds(pl.multiple_of((1 - core if other else core) * half, half), half)
    owner = member_ref[tokens, :]
    lane = lax.broadcasted_iota(I32, (half, 128), 1)

    def own(full):
        total = jnp.zeros((half, 128), F32)
        for j in range(POLICIES // 2):
            mine = owner == 2 * j + jnp.where(lane >= RANK, 1, 0)
            total = total + jnp.where(mine, full[:, j * 128 : (j + 1) * 128], 0.0)
        return total + pltpu.roll(total, RANK, 1)

    wait(slice(5, 7))
    low_out = own(
        lax.dot_general(cot_ref[tokens, :], up_ref[...], (((1,), (1,)), ((), ())), preferred_element_type=F32)
    )
    wait(slice(7, 9))
    low_in = jnp.dot(acts_ref[tokens, :CUT], down_ref[:CUT, :], preferred_element_type=F32)
    wait(slice(9, 11))
    low_in = own(low_in + jnp.dot(acts_ref[tokens, CUT:], down_ref[CUT:, :], preferred_element_type=F32))
    out_ref[...] = jnp.where(lane < RANK, low_in, low_out) * weight_ref[tokens, :]


def keep_kernel(acts_ref, cot_ref, down_ref, up_ref, member_ref, weight_ref, out_ref):
    half_products(False, acts_ref, cot_ref, down_ref, up_ref, member_ref, weight_ref, out_ref, lambda group: None)


BLOCKS = 4
NEAR = 4


def pack_kernel(keep_ref, got_ref, sum_ref, out_ref):
    half = keep_ref.shape[0]
    step = half // BLOCKS
    total = keep_ref[...] + got_ref[...]
    sum_ref[...] = total
    codes = []
    for b in range(BLOCKS):
        part = total[b * step : (b + 1) * step]
        code = code_of(jnp.max(jnp.abs(part), axis=0, keepdims=True))
        codes.append(code)
        out_ref[b * step : (b + 1) * step, :] = to_i16(part * (TOP / scale_of(code)))
    codes.append(jnp.zeros((16 - BLOCKS, 128), F32))
    out_ref[half:, :] = jnp.concatenate(codes, axis=0).astype(I32).astype(I16)


def unpack_kernel(sum_ref, got_ref, out_ref):
    half = sum_ref.shape[0]
    step = half // BLOCKS
    scale = scale_of(from_i16(got_ref[half:, :])) * (1.0 / TOP)
    for b in range(BLOCKS):
        at = slice(b * step, (b + 1) * step)
        out_ref[at, :] = sum_ref[at, :] + from_i16(got_ref[at, :]) * scale[b : b + 1]


def quantize(values_a, values_b):
    code_a = code_of(jnp.max(jnp.abs(values_a), axis=1, keepdims=True))
    code_b = code_of(jnp.max(jnp.abs(values_b), axis=1, keepdims=True))
    lane = lax.broadcasted_iota(I32, (values_a.shape[0], 128), 1)
    codes = jnp.where(lane == 0, code_a, code_b)
    inverse = TOP / scale_of(codes)
    q_a = to_i16(values_a * inverse[:, 0:1])
    q_b = to_i16(values_b * inverse[:, 1:2])
    return q_a, q_b, codes


def half_gradients(other, owner_ref, half_ref, acts_ref, cot_ref, low_ref, left_ref, store):
    half = half_ref.shape[0]
    core = lax.rem(lax.axis_index("mp"), 2)
    tokens = pl.ds(pl.multiple_of((1 - core if other else core) * half, half), half)
    low = half_ref[...].T
    high = low.astype(BF16).astype(F32)
    low_ref[0] = high
    low_ref[1] = low - high
    mask = owner_ref[:, tokens] == lax.broadcasted_iota(I32, (POLICIES, half), 0)
    for side, first_rank in ((0, RANK), (1, 0)):
        for part in range(2):
            for k in range(4):
                for d in range(4):
                    start = first_rank + jnp.where(core == 0, k * 16 + d * 4, d * 16 + k * 4)
                    at = part * 256 + (k % 2) * 128 + d * 32
                    rows = []
                    for i in range(4):
                        row = low_ref[part, pl.ds(start + i, 1), :]
                        rows.append(jnp.where(mask, jnp.broadcast_to(row, mask.shape), 0.0))
                    left_ref[side, k // 2, at : at + 32, :] = jnp.concatenate(rows, axis=0).astype(BF16)
    for h in range(2):
        rows, at = slice(h * 256, (h + 1) * 256), 0
        for side, x_ref in ((0, acts_ref), (1, cot_ref)):
            left = left_ref[side, h]
            width = x_ref.shape[1]
            for c0 in range(0, width, 256):
                c1 = min(c0 + 256, width)
                both = jnp.dot(left, x_ref[tokens, c0:c1], preferred_element_type=F32)
                store(rows, slice(at + c0, at + c1), both[:256] + both[256:])
            at += width
        yield h


def own_kernel(owner_ref, half_ref, acts_ref, cot_ref, sum_ref, low_ref, left_ref):
    def store(rows, columns, values):
        sum_ref[rows, columns] = values

    for _ in half_gradients(False, owner_ref, half_ref, acts_ref, cot_ref, low_ref, left_ref, store):
        pass


def grad_kernel(owner_ref, half_ref, acts_ref, cot_ref, sum_ref, out_ref, low_ref, left_ref, f_ref):
    wide_a, wide_b = acts_ref.shape[1], cot_ref.shape[1]
    quarter = full_rows(out_ref, wide_a + wide_b)

    def store(rows, columns, values):
        f_ref[rows, columns] = values + sum_ref[rows, columns]

    for h in half_gradients(True, owner_ref, half_ref, acts_ref, cot_ref, low_ref, left_ref, store):
        for k in (2 * h, 2 * h + 1):
            at = slice(k * quarter, (k + 1) * quarter)
            q_a, q_b, codes = quantize(f_ref[at, :wide_a], f_ref[at, wide_a:])
            store_columns(out_ref, k, q_a, q_b)
            out_ref[k, -16:, :] = codes.T[:16].astype(I32).astype(I16)


def full_rows(ref, width):
    return (ref.shape[1] - 16) // (width // 128)


def store_columns(out_ref, k, q_a, q_b):
    rows, at = q_a.shape[0], 0
    for q in (q_a, q_b):
        for c in range(0, q.shape[1], 128):
            out_ref[k, at : at + rows, :] = q[:, c : c + 128]
            at += rows


def sum_parts(scales, parts):
    total_a = total_b = None
    for (s_a, s_b), (a, b) in zip(scales, parts):
        a, b = from_i16(a) * s_a, from_i16(b) * s_b
        total_a = a if total_a is None else total_a + a
        total_b = b if total_b is None else total_b + b
    return total_a, total_b


def second_kernel(wide_a, wide_b, got_ref, out_ref):
    rows = full_rows(got_ref, wide_a + wide_b)
    n_a, n_b = wide_a // 128, wide_b // 128
    scales = []
    for k in range(4):
        codes = from_i16(got_ref[k, -16:, :])
        codes = scale_of(jnp.concatenate([codes, jnp.zeros((112, 128), F32)], axis=0).T) * (1.0 / TOP)
        scales.append((codes[:, 0:1], codes[:, 1:2]))

    def column(c):
        total = None
        for k in range(4):
            part = from_i16(got_ref[k, c * rows : (c + 1) * rows, :]) * scales[k][0 if c < n_a else 1]
            total = part if total is None else total + part
        return total

    total_a = jnp.concatenate([column(c) for c in range(n_a)], axis=1)
    total_b = jnp.concatenate([column(c) for c in range(n_a, n_a + n_b)], axis=1)
    q_a, q_b, codes = quantize(total_a, total_b)
    codes = codes.astype(I32).astype(I16)
    rows = out_ref.shape[1]
    for k in range(4):
        at = slice(k * rows, (k + 1) * rows)
        out_ref[k, :, :wide_a] = q_a[at]
        out_ref[k, :, wide_a : wide_a + wide_b] = q_b[at]
        out_ref[k, :, wide_a + wide_b :] = codes[at]


def third_kernel(wide_a, wide_b, got_ref, out_ref, total_ref):
    parts, scales = [], []
    for k in range(4):
        codes = scale_of(from_i16(got_ref[k, :, wide_a + wide_b :])) * (1.0 / TOP)
        scales.append((codes[:, 0:1], codes[:, 1:2]))
        parts.append((got_ref[k, :, :wide_a], got_ref[k, :, wide_a : wide_a + wide_b]))
    total_a, total_b = sum_parts(scales, parts)
    n_a, n_b = wide_a // 128, wide_b // 128
    for c in range(n_a):
        total_ref[c * 32 : (c + 1) * 32, :] = total_a[:, c * 128 : (c + 1) * 128]
    for c in range(n_b):
        total_ref[(n_a + c) * 32 : (n_a + c + 1) * 32, :] = total_b[:, c * 128 : (c + 1) * 128]

    def code_for(parts):
        most = jnp.abs(parts[0])
        for part in parts[1:]:
            most = jnp.maximum(most, jnp.abs(part))
        return code_of(jnp.max(jnp.max(most, axis=0, keepdims=True), axis=1, keepdims=True))

    def piece_of(p):
        parts = [total_ref[pl.ds(c * 32 + p, 4, stride=POLICIES), :] for c in range(n_a + n_b)]
        code_a, code_b = code_for(parts[:n_a]), code_for(parts[n_a:])
        pieces = [part * (TOP / scale_of(code_a)) for part in parts[:n_a]]
        pieces += [part * (TOP / scale_of(code_b)) for part in parts[n_a:]]
        row = lax.broadcasted_iota(I32, (4, 128), 0)
        return pieces + [jnp.where(row == 0, code_a, code_b)]

    for m in range(NEAR):
        pieces = []
        for p in range(m, POLICIES, NEAR):
            pieces += piece_of(p)
        out_ref[m] = to_i16(jnp.concatenate(pieces, axis=0))


def open_piece(values, n_a, n_b):
    at = 4 * (n_a + n_b)
    s_a = scale_of(values[at : at + 1]) * (1.0 / TOP)
    s_b = scale_of(values[at + 1 : at + 2]) * (1.0 / TOP)
    row = lax.broadcasted_iota(I32, values.shape, 0)
    return values * jnp.where(row < 4 * n_a, s_a, s_b)


def fourth_kernel(wide_a, wide_b, got_ref, mine_ref, out_ref):
    n_a, n_b = wide_a // 128, wide_b // 128
    deep = 4 * (n_a + n_b) + 4
    low = high = None
    for k in range(NEAR):
        values = from_i16(got_ref[k])
        first, second = open_piece(values[:deep], n_a, n_b), open_piece(values[deep:], n_a, n_b)
        low = first if low is None else low + first
        high = second if high is None else high + second
    upper = lax.axis_index("dp") // 16 >= NEAR
    mine_ref[...] = jnp.where(upper, high, low)
    other = jnp.where(upper, low, high)
    row = lax.broadcasted_iota(I32, other.shape, 0)

    def code_for(first, last):
        most = jnp.where((row >= first) & (row < last), jnp.abs(other), 0.0)
        return code_of(jnp.max(jnp.max(most, axis=0, keepdims=True), axis=1, keepdims=True))

    code_a, code_b = code_for(0, 4 * n_a), code_for(4 * n_a, deep - 4)
    values = other * jnp.where(row < 4 * n_a, TOP / scale_of(code_a), TOP / scale_of(code_b))
    values = jnp.where(row < deep - 4, values, jnp.where(row == deep - 4, code_a, code_b))
    out_ref[...] = to_i16(jnp.concatenate([values, jnp.zeros((8, 128), F32)], axis=0))


def last_kernel(wide_a, wide_b, mine_ref, got_ref, a_ref, b_ref):
    n_a, n_b = wide_a // 128, wide_b // 128
    values = from_i16(got_ref[...])[: mine_ref.shape[0]]
    total = mine_ref[...] + open_piece(values, n_a, n_b)
    for c in range(n_a):
        a_ref[:, c * 128 : (c + 1) * 128] = total[c * 4 : (c + 1) * 4]
    for c in range(n_b):
        b_ref[:, c * 128 : (c + 1) * 128] = total[4 * (n_a + c) : 4 * (n_a + c + 1)]


def call(kernel, outs, spaces, scratch=()):
    return pl.pallas_call(
        kernel,
        out_shape=[jax.ShapeDtypeStruct(s, d) for s, d in outs],
        in_specs=[pl.BlockSpec(memory_space=m) for m in spaces],
        out_specs=[pl.BlockSpec(memory_space=pltpu.VMEM)] * len(outs),
        scratch_shapes=list(scratch),
        compiler_params=pltpu.CompilerParams(vmem_limit_bytes=40 * 1024 * 1024),
    )


def in_hbm(array):
    return pltpu.with_memory_space_constraint(array, pltpu.HBM)


def groups_of():
    index = np.arange(512).reshape(8, 4, 4, 2, 2)
    first, second = [], []
    for z in range(8):
        for h in range(2):
            for k in range(4):
                first.append(index[z, :, k, h, 0].tolist())
                first.append(index[z, k, :, h, 1].tolist())
                second.append(index[z, k, :, h, 0].tolist())
                second.append(index[z, :, k, h, 1].tolist())
    third = [
        index[z : z + NEAR, x, y, h, c].tolist()
        for z in (0, NEAR)
        for x in range(4)
        for y in range(4)
        for h in range(2)
        for c in range(2)
    ]
    return first, second, third


def shards(acts, cot, lengths, policy, advantages, old, new, down, up):
    tokens, wide_a = acts.shape
    wide_b = cot.shape[1]
    half = tokens // 2
    first, second, third = groups_of()
    core_pairs = [(0, 1), (1, 0), (2, 3), (3, 2)]
    far_pairs = [(0, 2), (2, 0), (1, 3), (3, 1)]
    lines = (tokens // 128, 128)
    send, owner, acts, cot, down, up, member, weight = call(
        low_kernel,
        [
            ((half, 128), F32),
            ((POLICIES, tokens), I32),
            (acts.shape, BF16),
            (cot.shape, BF16),
            (down.shape, BF16),
            (up.shape, BF16),
            ((tokens, 128), I32),
            ((tokens, 128), F32),
        ],
        [HBM] * 9,
        [
            SMEM(lengths.shape, I32),
            SMEM(policy.shape, I32),
            SMEM(advantages.shape, F32),
            VMEM(lines, F32),
            VMEM(lines, F32),
            pltpu.SemaphoreType.DMA((11,)),
        ],
    )(*map(in_hbm, (lengths, policy, advantages, old.reshape(lines), new.reshape(lines), acts, cot, down, up)))
    got = lax.ppermute(send, "mp", core_pairs)
    (keep,) = call(keep_kernel, [((half, 128), F32)], [VMEM] * 6)(acts, cot, down, up, member, weight)
    part, packed = call(pack_kernel, [((half, 128), F32), ((half + 16, 128), I16)], [VMEM] * 2)(keep, got)
    far = lax.ppermute(packed, "mp", far_pairs)
    (mine,) = call(unpack_kernel, [((half, 128), F32)], [VMEM] * 2)(part, far)
    other = lax.ppermute(mine, "mp", core_pairs)
    rows = POLICIES * RANK
    width = wide_a + wide_b + 128
    scratch = [VMEM((2, 2 * RANK, half), F32), VMEM((2, 2, rows, half), BF16)]
    total = ((rows, wide_a + wide_b), F32)
    (own,) = call(own_kernel, [total], [VMEM] * 4, scratch)(owner, mine, acts, cot)
    (pieces,) = call(
        grad_kernel,
        [((4, rows // 4 * (wide_a + wide_b) // 128 + 16, 128), I16)],
        [VMEM] * 5,
        scratch + [VMEM(*total)],
    )(owner, other, acts, cot, own)
    got = lax.all_to_all(pieces, BOTH, 0, 0, tiled=True, axis_index_groups=first)
    (pieces,) = call(
        functools.partial(second_kernel, wide_a, wide_b), [((4, rows // 16, width), I16)], [VMEM]
    )(got)
    got = lax.all_to_all(pieces, BOTH, 0, 0, tiled=True, axis_index_groups=second)
    deep = 4 * (wide_a + wide_b) // 128 + 4
    (pieces,) = call(
        functools.partial(third_kernel, wide_a, wide_b), [((NEAR, 2 * deep, 128), I16)], [VMEM], [VMEM((rows // 16 * (wide_a + wide_b) // 128, 128), F32)]
    )(got)
    got = lax.all_to_all(pieces, BOTH, 0, 0, tiled=True, axis_index_groups=third)
    part, packed = call(
        functools.partial(fourth_kernel, wide_a, wide_b),
        [((deep, 128), F32), ((deep + 8, 128), I16)],
        [VMEM],
    )(got)
    count = lax.axis_size("dp")
    got = lax.ppermute(packed, "dp", [(i, (i + count // 2) % count) for i in range(count)])
    return tuple(
        call(
            functools.partial(last_kernel, wide_a, wide_b), [((4, wide_a), F32), ((4, wide_b), F32)], [VMEM] * 2
        )(part, got)
    )


def solution(mesh):
    return jax.shard_map(
        shards,
        mesh=mesh,
        in_specs=(
            P("dp", "mp"),
            P("dp", "mp"),
            P("dp", None),
            P("dp", None),
            P("dp", None),
            P("dp"),
            P("dp"),
            P("mp", None),
            P(None, "mp"),
        ),
        out_specs=(P("dp", "mp"), P("dp", "mp")),
        check_vma=False,
    )
```

```python
import functools

import jax
import jax.numpy as jnp
import numpy as np
from jax import lax
from jax.experimental import pallas as pl
from jax.experimental.pallas import tpu as pltpu
from jax.sharding import PartitionSpec as P

RANK = 64
POLICIES = 8
SEQS = 8
ADAPTER_SCALE = 2.0
CLIP_LOW = 0.8
CLIP_HIGH = 1.28
TINY = 1e-30
TOP = 32767.0
F32, BF16, I16, I32 = jnp.float32, jnp.bfloat16, jnp.int16, jnp.int32
BOTH = ("dp", "mp")
VMEM, SMEM, HBM = pltpu.VMEM, pltpu.SMEM, pltpu.HBM


def code_of(largest):
    return jnp.ceil(jnp.log2(jnp.maximum(largest, TINY)) * 256.0) + 1.0


def scale_of(code):
    return jnp.exp2(code * (1.0 / 256.0))


def to_i16(values):
    return jnp.round(values).astype(I32).astype(I16)


def from_i16(values):
    return values.astype(I32).astype(F32)


def starts_of(lengths_ref):
    bounds = [jnp.int32(0)]
    for s in range(SEQS):
        bounds.append(bounds[-1] + lengths_ref[0, s])
    return bounds


CUT = 512


def low_kernel(
    lengths_hbm, policy_hbm, adv_hbm, old_hbm, new_hbm, acts_hbm, cot_hbm, down_hbm, up_hbm,
    send_ref, owner_ref, acts_ref, cot_ref, down_ref, up_ref, member_ref, weight_ref,
    lengths_ref, policy_ref, adv_ref, old_ref, new_ref, sems,
):
    tokens, wide_a = acts_ref.shape
    half = tokens // 2
    core = lax.rem(lax.axis_index("mp"), 2)
    sent = pl.ds(pl.multiple_of((1 - core) * half, half), half)
    kept = pl.ds(pl.multiple_of(core * half, half), half)
    pairs = [
        (lengths_hbm, lengths_ref),
        (policy_hbm, policy_ref),
        (adv_hbm, adv_ref),
        (old_hbm, old_ref),
        (new_hbm, new_ref),
        (cot_hbm.at[sent, :], cot_ref.at[sent, :]),
        (up_hbm, up_ref),
        (acts_hbm.at[sent, :CUT], acts_ref.at[sent, :CUT]),
        (down_hbm.at[:CUT, :], down_ref.at[:CUT, :]),
        (acts_hbm.at[sent, CUT:], acts_ref.at[sent, CUT:]),
        (down_hbm.at[CUT:, :], down_ref.at[CUT:, :]),
        (cot_hbm.at[kept, :], cot_ref.at[kept, :]),
        (acts_hbm.at[kept, :], acts_ref.at[kept, :]),
    ]
    copies = [pltpu.make_async_copy(src, dst, sems.at[i]) for i, (src, dst) in enumerate(pairs)]
    for copy in copies:
        copy.start()
    for copy in copies[:5]:
        copy.wait()
    bounds = starts_of(lengths_ref)
    row = lax.broadcasted_iota(I32, (tokens, 128), 0)
    lane = lax.broadcasted_iota(I32, (tokens, 128), 1)
    owner = jnp.full((tokens, 128), -1, I32)
    factor = jnp.zeros((tokens, 128), F32)
    for s in range(SEQS):
        inside = (row >= bounds[s]) & (row < bounds[s + 1])
        total = jnp.full((8, 128), adv_ref[0, s], F32) / jnp.full((8, 128), lengths_ref[0, s], I32).astype(F32)
        owner = jnp.where(inside, policy_ref[0, s], owner)
        factor = jnp.where(inside, total[0:1, :], factor)
    pos = lax.broadcasted_iota(I32, (POLICIES, tokens), 1)
    held = jnp.full((POLICIES, tokens), -1, I32)
    for s in range(SEQS):
        held = jnp.where((pos >= bounds[s]) & (pos < bounds[s + 1]), policy_ref[0, s], held)
    owner_ref[...] = held
    ratio = jnp.clip(jnp.exp(new_ref[...] - old_ref[...]), CLIP_LOW, CLIP_HIGH) * ADAPTER_SCALE
    groups = ratio.shape[0]
    ratio = jnp.concatenate([ratio, jnp.zeros((128 - groups, 128), F32)], axis=0).T
    ratio = jnp.concatenate([ratio[:, j : j + 1] for j in range(groups)], axis=0)
    weight_ref[...] = factor * ratio
    member_ref[...] = owner

    def wait(group):
        for copy in copies[group]:
            copy.wait()

    half_products(True, acts_ref, cot_ref, down_ref, up_ref, member_ref, weight_ref, send_ref, wait)
    wait(slice(11, 13))


def half_products(other, acts_ref, cot_ref, down_ref, up_ref, member_ref, weight_ref, out_ref, wait):
    half = out_ref.shape[0]
    core = lax.rem(lax.axis_index("mp"), 2)
    tokens = pl.ds(pl.multiple_of((1 - core if other else core) * half, half), half)
    owner = member_ref[tokens, :]
    lane = lax.broadcasted_iota(I32, (half, 128), 1)

    def own(full):
        total = jnp.zeros((half, 128), F32)
        for j in range(POLICIES // 2):
            mine = owner == 2 * j + jnp.where(lane >= RANK, 1, 0)
            total = total + jnp.where(mine, full[:, j * 128 : (j + 1) * 128], 0.0)
        return total + pltpu.roll(total, RANK, 1)

    wait(slice(5, 7))
    low_out = own(
        lax.dot_general(cot_ref[tokens, :], up_ref[...], (((1,), (1,)), ((), ())), preferred_element_type=F32)
    )
    wait(slice(7, 9))
    low_in = jnp.dot(acts_ref[tokens, :CUT], down_ref[:CUT, :], preferred_element_type=F32)
    wait(slice(9, 11))
    low_in = own(low_in + jnp.dot(acts_ref[tokens, CUT:], down_ref[CUT:, :], preferred_element_type=F32))
    out_ref[...] = jnp.where(lane < RANK, low_in, low_out) * weight_ref[tokens, :]


def keep_kernel(acts_ref, cot_ref, down_ref, up_ref, member_ref, weight_ref, out_ref):
    half_products(False, acts_ref, cot_ref, down_ref, up_ref, member_ref, weight_ref, out_ref, lambda group: None)


BLOCKS = 4
NEAR = 4


def pack_kernel(keep_ref, got_ref, sum_ref, out_ref):
    half = keep_ref.shape[0]
    step = half // BLOCKS
    total = keep_ref[...] + got_ref[...]
    sum_ref[...] = total
    codes = []
    for b in range(BLOCKS):
        part = total[b * step : (b + 1) * step]
        code = code_of(jnp.max(jnp.abs(part), axis=0, keepdims=True))
        codes.append(code)
        out_ref[b * step : (b + 1) * step, :] = to_i16(part * (TOP / scale_of(code)))
    codes.append(jnp.zeros((16 - BLOCKS, 128), F32))
    out_ref[half:, :] = jnp.concatenate(codes, axis=0).astype(I32).astype(I16)


def unpack_kernel(sum_ref, got_ref, out_ref):
    half = sum_ref.shape[0]
    step = half // BLOCKS
    scale = scale_of(from_i16(got_ref[half:, :])) * (1.0 / TOP)
    for b in range(BLOCKS):
        at = slice(b * step, (b + 1) * step)
        out_ref[at, :] = sum_ref[at, :] + from_i16(got_ref[at, :]) * scale[b : b + 1]


def quantize(values_a, values_b):
    code_a = code_of(jnp.max(jnp.abs(values_a), axis=1, keepdims=True))
    code_b = code_of(jnp.max(jnp.abs(values_b), axis=1, keepdims=True))
    lane = lax.broadcasted_iota(I32, (values_a.shape[0], 128), 1)
    codes = jnp.where(lane == 0, code_a, code_b)
    inverse = TOP / scale_of(codes)
    q_a = to_i16(values_a * inverse[:, 0:1])
    q_b = to_i16(values_b * inverse[:, 1:2])
    return q_a, q_b, codes


def half_gradients(other, owner_ref, half_ref, acts_ref, cot_ref, low_ref, left_ref, store):
    half = half_ref.shape[0]
    core = lax.rem(lax.axis_index("mp"), 2)
    tokens = pl.ds(pl.multiple_of((1 - core if other else core) * half, half), half)
    low = half_ref[...].T
    high = low.astype(BF16).astype(F32)
    low_ref[0] = high
    low_ref[1] = low - high
    mask = owner_ref[:, tokens] == lax.broadcasted_iota(I32, (POLICIES, half), 0)
    for side, first_rank in ((0, RANK), (1, 0)):
        for part in range(2):
            for k in range(4):
                for d in range(4):
                    start = first_rank + jnp.where(core == 0, k * 16 + d * 4, d * 16 + k * 4)
                    at = part * 256 + (k % 2) * 128 + d * 32
                    rows = []
                    for i in range(4):
                        row = low_ref[part, pl.ds(start + i, 1), :]
                        rows.append(jnp.where(mask, jnp.broadcast_to(row, mask.shape), 0.0))
                    left_ref[side, k // 2, at : at + 32, :] = jnp.concatenate(rows, axis=0).astype(BF16)
    for h in range(2):
        rows, at = slice(h * 256, (h + 1) * 256), 0
        for side, x_ref in ((0, acts_ref), (1, cot_ref)):
            left = left_ref[side, h]
            width = x_ref.shape[1]
            for c0 in range(0, width, 256):
                c1 = min(c0 + 256, width)
                both = jnp.dot(left, x_ref[tokens, c0:c1], preferred_element_type=F32)
                store(rows, slice(at + c0, at + c1), both[:256] + both[256:])
            at += width
        yield h


def own_kernel(owner_ref, half_ref, acts_ref, cot_ref, sum_ref, low_ref, left_ref):
    def store(rows, columns, values):
        sum_ref[rows, columns] = values

    for _ in half_gradients(False, owner_ref, half_ref, acts_ref, cot_ref, low_ref, left_ref, store):
        pass


def grad_kernel(owner_ref, half_ref, acts_ref, cot_ref, sum_ref, out_ref, low_ref, left_ref, f_ref):
    wide_a, wide_b = acts_ref.shape[1], cot_ref.shape[1]
    quarter = full_rows(out_ref, wide_a + wide_b)

    def store(rows, columns, values):
        f_ref[rows, columns] = values + sum_ref[rows, columns]

    for h in half_gradients(True, owner_ref, half_ref, acts_ref, cot_ref, low_ref, left_ref, store):
        for k in (2 * h, 2 * h + 1):
            at = slice(k * quarter, (k + 1) * quarter)
            q_a, q_b, codes = quantize(f_ref[at, :wide_a], f_ref[at, wide_a:])
            store_columns(out_ref, k, q_a, q_b)
            out_ref[k, -16:, :] = codes.T[:16].astype(I32).astype(I16)


def full_rows(ref, width):
    return (ref.shape[1] - 16) // (width // 128)


def store_columns(out_ref, k, q_a, q_b):
    rows, at = q_a.shape[0], 0
    for q in (q_a, q_b):
        for c in range(0, q.shape[1], 128):
            out_ref[k, at : at + rows, :] = q[:, c : c + 128]
            at += rows


def sum_parts(scales, parts):
    total_a = total_b = None
    for (s_a, s_b), (a, b) in zip(scales, parts):
        a, b = from_i16(a) * s_a, from_i16(b) * s_b
        total_a = a if total_a is None else total_a + a
        total_b = b if total_b is None else total_b + b
    return total_a, total_b


def second_kernel(wide_a, wide_b, got_ref, out_ref):
    rows = full_rows(got_ref, wide_a + wide_b)
    n_a, n_b = wide_a // 128, wide_b // 128
    scales = []
    for k in range(4):
        codes = from_i16(got_ref[k, -16:, :])
        codes = scale_of(jnp.concatenate([codes, jnp.zeros((112, 128), F32)], axis=0).T) * (1.0 / TOP)
        scales.append((codes[:, 0:1], codes[:, 1:2]))

    def column(c):
        total = None
        for k in range(4):
            part = from_i16(got_ref[k, c * rows : (c + 1) * rows, :]) * scales[k][0 if c < n_a else 1]
            total = part if total is None else total + part
        return total

    total_a = jnp.concatenate([column(c) for c in range(n_a)], axis=1)
    total_b = jnp.concatenate([column(c) for c in range(n_a, n_a + n_b)], axis=1)
    q_a, q_b, codes = quantize(total_a, total_b)
    codes = codes.astype(I32).astype(I16)
    rows = out_ref.shape[1]
    for k in range(4):
        at = slice(k * rows, (k + 1) * rows)
        out_ref[k, :, :wide_a] = q_a[at]
        out_ref[k, :, wide_a : wide_a + wide_b] = q_b[at]
        out_ref[k, :, wide_a + wide_b :] = codes[at]


def third_kernel(wide_a, wide_b, got_ref, out_ref, total_ref):
    parts, scales = [], []
    for k in range(4):
        codes = scale_of(from_i16(got_ref[k, :, wide_a + wide_b :])) * (1.0 / TOP)
        scales.append((codes[:, 0:1], codes[:, 1:2]))
        parts.append((got_ref[k, :, :wide_a], got_ref[k, :, wide_a : wide_a + wide_b]))
    total_a, total_b = sum_parts(scales, parts)
    n_a, n_b = wide_a // 128, wide_b // 128
    for c in range(n_a):
        total_ref[c * 32 : (c + 1) * 32, :] = total_a[:, c * 128 : (c + 1) * 128]
    for c in range(n_b):
        total_ref[(n_a + c) * 32 : (n_a + c + 1) * 32, :] = total_b[:, c * 128 : (c + 1) * 128]

    def code_for(parts):
        most = jnp.abs(parts[0])
        for part in parts[1:]:
            most = jnp.maximum(most, jnp.abs(part))
        return code_of(jnp.max(jnp.max(most, axis=0, keepdims=True), axis=1, keepdims=True))

    def piece_of(p):
        parts = [total_ref[pl.ds(c * 32 + p, 4, stride=POLICIES), :] for c in range(n_a + n_b)]
        code_a, code_b = code_for(parts[:n_a]), code_for(parts[n_a:])
        pieces = [part * (TOP / scale_of(code_a)) for part in parts[:n_a]]
        pieces += [part * (TOP / scale_of(code_b)) for part in parts[n_a:]]
        row = lax.broadcasted_iota(I32, (4, 128), 0)
        return pieces + [jnp.where(row == 0, code_a, code_b)]

    for m in range(NEAR):
        pieces = []
        for p in range(m, POLICIES, NEAR):
            pieces += piece_of(p)
        out_ref[m] = to_i16(jnp.concatenate(pieces, axis=0))


def open_piece(values, n_a, n_b):
    at = 4 * (n_a + n_b)
    s_a = scale_of(values[at : at + 1]) * (1.0 / TOP)
    s_b = scale_of(values[at + 1 : at + 2]) * (1.0 / TOP)
    row = lax.broadcasted_iota(I32, values.shape, 0)
    return values * jnp.where(row < 4 * n_a, s_a, s_b)


def fourth_kernel(wide_a, wide_b, got_ref, mine_ref, out_ref):
    n_a, n_b = wide_a // 128, wide_b // 128
    deep = 4 * (n_a + n_b) + 4
    low = high = None
    for k in range(NEAR):
        values = from_i16(got_ref[k])
        first, second = open_piece(values[:deep], n_a, n_b), open_piece(values[deep:], n_a, n_b)
        low = first if low is None else low + first
        high = second if high is None else high + second
    upper = lax.axis_index("dp") // 16 >= NEAR
    mine_ref[...] = jnp.where(upper, high, low)
    other = jnp.where(upper, low, high)
    row = lax.broadcasted_iota(I32, other.shape, 0)

    def code_for(first, last):
        most = jnp.where((row >= first) & (row < last), jnp.abs(other), 0.0)
        return code_of(jnp.max(jnp.max(most, axis=0, keepdims=True), axis=1, keepdims=True))

    code_a, code_b = code_for(0, 4 * n_a), code_for(4 * n_a, deep - 4)
    values = other * jnp.where(row < 4 * n_a, TOP / scale_of(code_a), TOP / scale_of(code_b))
    values = jnp.where(row < deep - 4, values, jnp.where(row == deep - 4, code_a, code_b))
    out_ref[...] = to_i16(jnp.concatenate([values, jnp.zeros((8, 128), F32)], axis=0))


def last_kernel(wide_a, wide_b, mine_ref, got_ref, a_ref, b_ref):
    n_a, n_b = wide_a // 128, wide_b // 128
    values = from_i16(got_ref[...])[: mine_ref.shape[0]]
    total = mine_ref[...] + open_piece(values, n_a, n_b)
    for c in range(n_a):
        a_ref[:, c * 128 : (c + 1) * 128] = total[c * 4 : (c + 1) * 4]
    for c in range(n_b):
        b_ref[:, c * 128 : (c + 1) * 128] = total[4 * (n_a + c) : 4 * (n_a + c + 1)]


def call(kernel, outs, spaces, scratch=()):
    return pl.pallas_call(
        kernel,
        out_shape=[jax.ShapeDtypeStruct(s, d) for s, d in outs],
        in_specs=[pl.BlockSpec(memory_space=m) for m in spaces],
        out_specs=[pl.BlockSpec(memory_space=pltpu.VMEM)] * len(outs),
        scratch_shapes=list(scratch),
        compiler_params=pltpu.CompilerParams(vmem_limit_bytes=40 * 1024 * 1024),
    )


def in_hbm(array):
    return pltpu.with_memory_space_constraint(array, pltpu.HBM)


def groups_of():
    index = np.arange(512).reshape(8, 4, 4, 2, 2)
    first, second = [], []
    for z in range(8):
        for h in range(2):
            for k in range(4):
                first.append(index[z, :, k, h, 0].tolist())
                first.append(index[z, k, :, h, 1].tolist())
                second.append(index[z, k, :, h, 0].tolist())
                second.append(index[z, :, k, h, 1].tolist())
    third = [
        index[z : z + NEAR, x, y, h, c].tolist()
        for z in (0, NEAR)
        for x in range(4)
        for y in range(4)
        for h in range(2)
        for c in range(2)
    ]
    return first, second, third


def shards(acts, cot, lengths, policy, advantages, old, new, down, up):
    tokens, wide_a = acts.shape
    wide_b = cot.shape[1]
    half = tokens // 2
    first, second, third = groups_of()
    core_pairs = [(0, 1), (1, 0), (2, 3), (3, 2)]
    far_pairs = [(0, 2), (2, 0), (1, 3), (3, 1)]
    lines = (tokens // 128, 128)
    send, owner, acts, cot, down, up, member, weight = call(
        low_kernel,
        [
            ((half, 128), F32),
            ((POLICIES, tokens), I32),
            (acts.shape, BF16),
            (cot.shape, BF16),
            (down.shape, BF16),
            (up.shape, BF16),
            ((tokens, 128), I32),
            ((tokens, 128), F32),
        ],
        [HBM] * 9,
        [
            SMEM(lengths.shape, I32),
            SMEM(policy.shape, I32),
            SMEM(advantages.shape, F32),
            VMEM(lines, F32),
            VMEM(lines, F32),
            pltpu.SemaphoreType.DMA((13,)),
        ],
    )(*map(in_hbm, (lengths, policy, advantages, old.reshape(lines), new.reshape(lines), acts, cot, down, up)))
    got = lax.ppermute(send, "mp", core_pairs)
    (keep,) = call(keep_kernel, [((half, 128), F32)], [VMEM] * 6)(acts, cot, down, up, member, weight)
    part, packed = call(pack_kernel, [((half, 128), F32), ((half + 16, 128), I16)], [VMEM] * 2)(keep, got)
    far = lax.ppermute(packed, "mp", far_pairs)
    (mine,) = call(unpack_kernel, [((half, 128), F32)], [VMEM] * 2)(part, far)
    other = lax.ppermute(mine, "mp", core_pairs)
    rows = POLICIES * RANK
    width = wide_a + wide_b + 128
    scratch = [VMEM((2, 2 * RANK, half), F32), VMEM((2, 2, rows, half), BF16)]
    total = ((rows, wide_a + wide_b), F32)
    (own,) = call(own_kernel, [total], [VMEM] * 4, scratch)(owner, mine, acts, cot)
    (pieces,) = call(
        grad_kernel,
        [((4, rows // 4 * (wide_a + wide_b) // 128 + 16, 128), I16)],
        [VMEM] * 5,
        scratch + [VMEM(*total)],
    )(owner, other, acts, cot, own)
    got = lax.all_to_all(pieces, BOTH, 0, 0, tiled=True, axis_index_groups=first)
    (pieces,) = call(
        functools.partial(second_kernel, wide_a, wide_b), [((4, rows // 16, width), I16)], [VMEM]
    )(got)
    got = lax.all_to_all(pieces, BOTH, 0, 0, tiled=True, axis_index_groups=second)
    deep = 4 * (wide_a + wide_b) // 128 + 4
    (pieces,) = call(
        functools.partial(third_kernel, wide_a, wide_b), [((NEAR, 2 * deep, 128), I16)], [VMEM], [VMEM((rows // 16 * (wide_a + wide_b) // 128, 128), F32)]
    )(got)
    got = lax.all_to_all(pieces, BOTH, 0, 0, tiled=True, axis_index_groups=third)
    part, packed = call(
        functools.partial(fourth_kernel, wide_a, wide_b),
        [((deep, 128), F32), ((deep + 8, 128), I16)],
        [VMEM],
    )(got)
    count = lax.axis_size("dp")
    got = lax.ppermute(packed, "dp", [(i, (i + count // 2) % count) for i in range(count)])
    return tuple(
        call(
            functools.partial(last_kernel, wide_a, wide_b), [((4, wide_a), F32), ((4, wide_b), F32)], [VMEM] * 2
        )(part, got)
    )


def solution(mesh):
    return jax.shard_map(
        shards,
        mesh=mesh,
        in_specs=(
            P("dp", "mp"),
            P("dp", "mp"),
            P("dp", None),
            P("dp", None),
            P("dp", None),
            P("dp"),
            P("dp"),
            P("mp", None),
            P(None, "mp"),
        ),
        out_specs=(P("dp", "mp"), P("dp", "mp")),
        check_vma=False,
    )
```

```python
import functools

import jax
import jax.numpy as jnp
import numpy as np
from jax import lax
from jax.experimental import pallas as pl
from jax.experimental.pallas import tpu as pltpu
from jax.sharding import PartitionSpec as P

RANK = 64
POLICIES = 8
SEQS = 8
ADAPTER_SCALE = 2.0
CLIP_LOW = 0.8
CLIP_HIGH = 1.28
TINY = 1e-30
TOP = 32767.0
F32, BF16, I16, I32 = jnp.float32, jnp.bfloat16, jnp.int16, jnp.int32
BOTH = ("dp", "mp")
VMEM, SMEM, HBM = pltpu.VMEM, pltpu.SMEM, pltpu.HBM


def code_of(largest):
    return jnp.ceil(jnp.log2(jnp.maximum(largest, TINY)) * 256.0) + 1.0


def scale_of(code):
    return jnp.exp2(code * (1.0 / 256.0))


def to_i16(values):
    return jnp.round(values).astype(I32).astype(I16)


def from_i16(values):
    return values.astype(I32).astype(F32)


def starts_of(lengths_ref):
    bounds = [jnp.int32(0)]
    for s in range(SEQS):
        bounds.append(bounds[-1] + lengths_ref[0, s])
    return bounds


CUT = 768


def low_kernel(
    lengths_hbm, policy_hbm, adv_hbm, old_hbm, new_hbm, acts_hbm, cot_hbm, down_hbm, up_hbm,
    send_ref, owner_ref, acts_ref, cot_ref, down_ref, up_ref, member_ref, weight_ref,
    lengths_ref, policy_ref, adv_ref, old_ref, new_ref, sems,
):
    tokens, wide_a = acts_ref.shape
    half = tokens // 2
    core = lax.rem(lax.axis_index("mp"), 2)
    sent = pl.ds(pl.multiple_of((1 - core) * half, half), half)
    kept = pl.ds(pl.multiple_of(core * half, half), half)
    pairs = [
        (lengths_hbm, lengths_ref),
        (policy_hbm, policy_ref),
        (adv_hbm, adv_ref),
        (old_hbm, old_ref),
        (new_hbm, new_ref),
        (cot_hbm.at[sent, :], cot_ref.at[sent, :]),
        (up_hbm, up_ref),
        (acts_hbm.at[sent, :CUT], acts_ref.at[sent, :CUT]),
        (down_hbm.at[:CUT, :], down_ref.at[:CUT, :]),
        (acts_hbm.at[sent, CUT:], acts_ref.at[sent, CUT:]),
        (down_hbm.at[CUT:, :], down_ref.at[CUT:, :]),
        (cot_hbm.at[kept, :], cot_ref.at[kept, :]),
        (acts_hbm.at[kept, :], acts_ref.at[kept, :]),
    ]
    copies = [pltpu.make_async_copy(src, dst, sems.at[i]) for i, (src, dst) in enumerate(pairs)]
    for copy in copies:
        copy.start()
    for copy in copies[:5]:
        copy.wait()
    bounds = starts_of(lengths_ref)
    row = lax.broadcasted_iota(I32, (tokens, 128), 0)
    lane = lax.broadcasted_iota(I32, (tokens, 128), 1)
    owner = jnp.full((tokens, 128), -1, I32)
    factor = jnp.zeros((tokens, 128), F32)
    for s in range(SEQS):
        inside = (row >= bounds[s]) & (row < bounds[s + 1])
        total = jnp.full((8, 128), adv_ref[0, s], F32) / jnp.full((8, 128), lengths_ref[0, s], I32).astype(F32)
        owner = jnp.where(inside, policy_ref[0, s], owner)
        factor = jnp.where(inside, total[0:1, :], factor)
    pos = lax.broadcasted_iota(I32, (POLICIES, tokens), 1)
    held = jnp.full((POLICIES, tokens), -1, I32)
    for s in range(SEQS):
        held = jnp.where((pos >= bounds[s]) & (pos < bounds[s + 1]), policy_ref[0, s], held)
    owner_ref[...] = held
    ratio = jnp.clip(jnp.exp(new_ref[...] - old_ref[...]), CLIP_LOW, CLIP_HIGH) * ADAPTER_SCALE
    groups = ratio.shape[0]
    ratio = jnp.concatenate([ratio, jnp.zeros((128 - groups, 128), F32)], axis=0).T
    ratio = jnp.concatenate([ratio[:, j : j + 1] for j in range(groups)], axis=0)
    weight_ref[...] = factor * ratio
    member_ref[...] = owner

    def wait(group):
        for copy in copies[group]:
            copy.wait()

    half_products(True, acts_ref, cot_ref, down_ref, up_ref, member_ref, weight_ref, send_ref, wait)
    wait(slice(11, 13))


def half_products(other, acts_ref, cot_ref, down_ref, up_ref, member_ref, weight_ref, out_ref, wait):
    half = out_ref.shape[0]
    core = lax.rem(lax.axis_index("mp"), 2)
    tokens = pl.ds(pl.multiple_of((1 - core if other else core) * half, half), half)
    owner = member_ref[tokens, :]
    lane = lax.broadcasted_iota(I32, (half, 128), 1)

    def own(full):
        total = jnp.zeros((half, 128), F32)
        for j in range(POLICIES // 2):
            mine = owner == 2 * j + jnp.where(lane >= RANK, 1, 0)
            total = total + jnp.where(mine, full[:, j * 128 : (j + 1) * 128], 0.0)
        return total + pltpu.roll(total, RANK, 1)

    wait(slice(5, 7))
    low_out = own(
        lax.dot_general(cot_ref[tokens, :], up_ref[...], (((1,), (1,)), ((), ())), preferred_element_type=F32)
    )
    wait(slice(7, 9))
    low_in = jnp.dot(acts_ref[tokens, :CUT], down_ref[:CUT, :], preferred_element_type=F32)
    wait(slice(9, 11))
    low_in = own(low_in + jnp.dot(acts_ref[tokens, CUT:], down_ref[CUT:, :], preferred_element_type=F32))
    out_ref[...] = jnp.where(lane < RANK, low_in, low_out) * weight_ref[tokens, :]


def keep_kernel(acts_ref, cot_ref, down_ref, up_ref, member_ref, weight_ref, out_ref):
    half_products(False, acts_ref, cot_ref, down_ref, up_ref, member_ref, weight_ref, out_ref, lambda group: None)


BLOCKS = 4
NEAR = 4


def pack_kernel(keep_ref, got_ref, sum_ref, out_ref):
    half = keep_ref.shape[0]
    step = half // BLOCKS
    total = keep_ref[...] + got_ref[...]
    sum_ref[...] = total
    codes = []
    for b in range(BLOCKS):
        part = total[b * step : (b + 1) * step]
        code = code_of(jnp.max(jnp.abs(part), axis=0, keepdims=True))
        codes.append(code)
        out_ref[b * step : (b + 1) * step, :] = to_i16(part * (TOP / scale_of(code)))
    codes.append(jnp.zeros((16 - BLOCKS, 128), F32))
    out_ref[half:, :] = jnp.concatenate(codes, axis=0).astype(I32).astype(I16)


def unpack_kernel(sum_ref, got_ref, out_ref):
    half = sum_ref.shape[0]
    step = half // BLOCKS
    scale = scale_of(from_i16(got_ref[half:, :])) * (1.0 / TOP)
    for b in range(BLOCKS):
        at = slice(b * step, (b + 1) * step)
        out_ref[at, :] = sum_ref[at, :] + from_i16(got_ref[at, :]) * scale[b : b + 1]


def quantize(values_a, values_b):
    code_a = code_of(jnp.max(jnp.abs(values_a), axis=1, keepdims=True))
    code_b = code_of(jnp.max(jnp.abs(values_b), axis=1, keepdims=True))
    lane = lax.broadcasted_iota(I32, (values_a.shape[0], 128), 1)
    codes = jnp.where(lane == 0, code_a, code_b)
    inverse = TOP / scale_of(codes)
    q_a = to_i16(values_a * inverse[:, 0:1])
    q_b = to_i16(values_b * inverse[:, 1:2])
    return q_a, q_b, codes


def half_gradients(other, owner_ref, half_ref, acts_ref, cot_ref, low_ref, left_ref, store):
    half = half_ref.shape[0]
    core = lax.rem(lax.axis_index("mp"), 2)
    tokens = pl.ds(pl.multiple_of((1 - core if other else core) * half, half), half)
    low = half_ref[...].T
    high = low.astype(BF16).astype(F32)
    low_ref[0] = high
    low_ref[1] = low - high
    mask = owner_ref[:, tokens] == lax.broadcasted_iota(I32, (POLICIES, half), 0)
    for side, first_rank in ((0, RANK), (1, 0)):
        for part in range(2):
            for k in range(4):
                for d in range(4):
                    start = first_rank + jnp.where(core == 0, k * 16 + d * 4, d * 16 + k * 4)
                    at = part * 256 + (k % 2) * 128 + d * 32
                    rows = []
                    for i in range(4):
                        row = low_ref[part, pl.ds(start + i, 1), :]
                        rows.append(jnp.where(mask, jnp.broadcast_to(row, mask.shape), 0.0))
                    left_ref[side, k // 2, at : at + 32, :] = jnp.concatenate(rows, axis=0).astype(BF16)
    for h in range(2):
        rows, at = slice(h * 256, (h + 1) * 256), 0
        for side, x_ref in ((0, acts_ref), (1, cot_ref)):
            left = left_ref[side, h]
            width = x_ref.shape[1]
            for c0 in range(0, width, 256):
                c1 = min(c0 + 256, width)
                both = jnp.dot(left, x_ref[tokens, c0:c1], preferred_element_type=F32)
                store(rows, slice(at + c0, at + c1), both[:256] + both[256:])
            at += width
        yield h


def own_kernel(owner_ref, half_ref, acts_ref, cot_ref, sum_ref, low_ref, left_ref):
    def store(rows, columns, values):
        sum_ref[rows, columns] = values

    for _ in half_gradients(False, owner_ref, half_ref, acts_ref, cot_ref, low_ref, left_ref, store):
        pass


def grad_kernel(owner_ref, half_ref, acts_ref, cot_ref, sum_ref, out_ref, low_ref, left_ref, f_ref):
    wide_a, wide_b = acts_ref.shape[1], cot_ref.shape[1]
    quarter = full_rows(out_ref, wide_a + wide_b)

    def store(rows, columns, values):
        f_ref[rows, columns] = values + sum_ref[rows, columns]

    for h in half_gradients(True, owner_ref, half_ref, acts_ref, cot_ref, low_ref, left_ref, store):
        for k in (2 * h, 2 * h + 1):
            at = slice(k * quarter, (k + 1) * quarter)
            q_a, q_b, codes = quantize(f_ref[at, :wide_a], f_ref[at, wide_a:])
            store_columns(out_ref, k, q_a, q_b)
            out_ref[k, -16:, :] = codes.T[:16].astype(I32).astype(I16)


def full_rows(ref, width):
    return (ref.shape[1] - 16) // (width // 128)


def store_columns(out_ref, k, q_a, q_b):
    rows, at = q_a.shape[0], 0
    for q in (q_a, q_b):
        for c in range(0, q.shape[1], 128):
            out_ref[k, at : at + rows, :] = q[:, c : c + 128]
            at += rows


def sum_parts(scales, parts):
    total_a = total_b = None
    for (s_a, s_b), (a, b) in zip(scales, parts):
        a, b = from_i16(a) * s_a, from_i16(b) * s_b
        total_a = a if total_a is None else total_a + a
        total_b = b if total_b is None else total_b + b
    return total_a, total_b


def second_kernel(wide_a, wide_b, got_ref, out_ref):
    rows = full_rows(got_ref, wide_a + wide_b)
    n_a, n_b = wide_a // 128, wide_b // 128
    scales = []
    for k in range(4):
        codes = from_i16(got_ref[k, -16:, :])
        codes = scale_of(jnp.concatenate([codes, jnp.zeros((112, 128), F32)], axis=0).T) * (1.0 / TOP)
        scales.append((codes[:, 0:1], codes[:, 1:2]))

    def column(c):
        total = None
        for k in range(4):
            part = from_i16(got_ref[k, c * rows : (c + 1) * rows, :]) * scales[k][0 if c < n_a else 1]
            total = part if total is None else total + part
        return total

    total_a = jnp.concatenate([column(c) for c in range(n_a)], axis=1)
    total_b = jnp.concatenate([column(c) for c in range(n_a, n_a + n_b)], axis=1)
    q_a, q_b, codes = quantize(total_a, total_b)
    codes = codes.astype(I32).astype(I16)
    rows = out_ref.shape[1]
    for k in range(4):
        at = slice(k * rows, (k + 1) * rows)
        out_ref[k, :, :wide_a] = q_a[at]
        out_ref[k, :, wide_a : wide_a + wide_b] = q_b[at]
        out_ref[k, :, wide_a + wide_b :] = codes[at]


def third_kernel(wide_a, wide_b, got_ref, out_ref, total_ref):
    parts, scales = [], []
    for k in range(4):
        codes = scale_of(from_i16(got_ref[k, :, wide_a + wide_b :])) * (1.0 / TOP)
        scales.append((codes[:, 0:1], codes[:, 1:2]))
        parts.append((got_ref[k, :, :wide_a], got_ref[k, :, wide_a : wide_a + wide_b]))
    total_a, total_b = sum_parts(scales, parts)
    n_a, n_b = wide_a // 128, wide_b // 128
    for c in range(n_a):
        total_ref[c * 32 : (c + 1) * 32, :] = total_a[:, c * 128 : (c + 1) * 128]
    for c in range(n_b):
        total_ref[(n_a + c) * 32 : (n_a + c + 1) * 32, :] = total_b[:, c * 128 : (c + 1) * 128]

    def code_for(parts):
        most = jnp.abs(parts[0])
        for part in parts[1:]:
            most = jnp.maximum(most, jnp.abs(part))
        return code_of(jnp.max(jnp.max(most, axis=0, keepdims=True), axis=1, keepdims=True))

    def piece_of(p):
        parts = [total_ref[pl.ds(c * 32 + p, 4, stride=POLICIES), :] for c in range(n_a + n_b)]
        code_a, code_b = code_for(parts[:n_a]), code_for(parts[n_a:])
        pieces = [part * (TOP / scale_of(code_a)) for part in parts[:n_a]]
        pieces += [part * (TOP / scale_of(code_b)) for part in parts[n_a:]]
        row = lax.broadcasted_iota(I32, (4, 128), 0)
        return pieces + [jnp.where(row == 0, code_a, code_b)]

    for m in range(NEAR):
        pieces = []
        for p in range(m, POLICIES, NEAR):
            pieces += piece_of(p)
        out_ref[m] = to_i16(jnp.concatenate(pieces, axis=0))


def open_piece(values, n_a, n_b):
    at = 4 * (n_a + n_b)
    s_a = scale_of(values[at : at + 1]) * (1.0 / TOP)
    s_b = scale_of(values[at + 1 : at + 2]) * (1.0 / TOP)
    row = lax.broadcasted_iota(I32, values.shape, 0)
    return values * jnp.where(row < 4 * n_a, s_a, s_b)


def fourth_kernel(wide_a, wide_b, got_ref, mine_ref, out_ref):
    n_a, n_b = wide_a // 128, wide_b // 128
    deep = 4 * (n_a + n_b) + 4
    low = high = None
    for k in range(NEAR):
        values = from_i16(got_ref[k])
        first, second = open_piece(values[:deep], n_a, n_b), open_piece(values[deep:], n_a, n_b)
        low = first if low is None else low + first
        high = second if high is None else high + second
    upper = lax.axis_index("dp") // 16 >= NEAR
    mine_ref[...] = jnp.where(upper, high, low)
    other = jnp.where(upper, low, high)
    row = lax.broadcasted_iota(I32, other.shape, 0)

    def code_for(first, last):
        most = jnp.where((row >= first) & (row < last), jnp.abs(other), 0.0)
        return code_of(jnp.max(jnp.max(most, axis=0, keepdims=True), axis=1, keepdims=True))

    code_a, code_b = code_for(0, 4 * n_a), code_for(4 * n_a, deep - 4)
    values = other * jnp.where(row < 4 * n_a, TOP / scale_of(code_a), TOP / scale_of(code_b))
    values = jnp.where(row < deep - 4, values, jnp.where(row == deep - 4, code_a, code_b))
    out_ref[...] = to_i16(jnp.concatenate([values, jnp.zeros((8, 128), F32)], axis=0))


def last_kernel(wide_a, wide_b, mine_ref, got_ref, a_ref, b_ref):
    n_a, n_b = wide_a // 128, wide_b // 128
    values = from_i16(got_ref[...])[: mine_ref.shape[0]]
    total = mine_ref[...] + open_piece(values, n_a, n_b)
    for c in range(n_a):
        a_ref[:, c * 128 : (c + 1) * 128] = total[c * 4 : (c + 1) * 4]
    for c in range(n_b):
        b_ref[:, c * 128 : (c + 1) * 128] = total[4 * (n_a + c) : 4 * (n_a + c + 1)]


def call(kernel, outs, spaces, scratch=()):
    return pl.pallas_call(
        kernel,
        out_shape=[jax.ShapeDtypeStruct(s, d) for s, d in outs],
        in_specs=[pl.BlockSpec(memory_space=m) for m in spaces],
        out_specs=[pl.BlockSpec(memory_space=pltpu.VMEM)] * len(outs),
        scratch_shapes=list(scratch),
        compiler_params=pltpu.CompilerParams(vmem_limit_bytes=40 * 1024 * 1024),
    )


def in_hbm(array):
    return pltpu.with_memory_space_constraint(array, pltpu.HBM)


def groups_of():
    index = np.arange(512).reshape(8, 4, 4, 2, 2)
    first, second = [], []
    for z in range(8):
        for h in range(2):
            for k in range(4):
                first.append(index[z, :, k, h, 0].tolist())
                first.append(index[z, k, :, h, 1].tolist())
                second.append(index[z, k, :, h, 0].tolist())
                second.append(index[z, :, k, h, 1].tolist())
    third = [
        index[z : z + NEAR, x, y, h, c].tolist()
        for z in (0, NEAR)
        for x in range(4)
        for y in range(4)
        for h in range(2)
        for c in range(2)
    ]
    return first, second, third


def shards(acts, cot, lengths, policy, advantages, old, new, down, up):
    tokens, wide_a = acts.shape
    wide_b = cot.shape[1]
    half = tokens // 2
    first, second, third = groups_of()
    core_pairs = [(0, 1), (1, 0), (2, 3), (3, 2)]
    far_pairs = [(0, 2), (2, 0), (1, 3), (3, 1)]
    lines = (tokens // 128, 128)
    send, owner, acts, cot, down, up, member, weight = call(
        low_kernel,
        [
            ((half, 128), F32),
            ((POLICIES, tokens), I32),
            (acts.shape, BF16),
            (cot.shape, BF16),
            (down.shape, BF16),
            (up.shape, BF16),
            ((tokens, 128), I32),
            ((tokens, 128), F32),
        ],
        [HBM] * 9,
        [
            SMEM(lengths.shape, I32),
            SMEM(policy.shape, I32),
            SMEM(advantages.shape, F32),
            VMEM(lines, F32),
            VMEM(lines, F32),
            pltpu.SemaphoreType.DMA((13,)),
        ],
    )(*map(in_hbm, (lengths, policy, advantages, old.reshape(lines), new.reshape(lines), acts, cot, down, up)))
    got = lax.ppermute(send, "mp", core_pairs)
    (keep,) = call(keep_kernel, [((half, 128), F32)], [VMEM] * 6)(acts, cot, down, up, member, weight)
    part, packed = call(pack_kernel, [((half, 128), F32), ((half + 16, 128), I16)], [VMEM] * 2)(keep, got)
    far = lax.ppermute(packed, "mp", far_pairs)
    (mine,) = call(unpack_kernel, [((half, 128), F32)], [VMEM] * 2)(part, far)
    other = lax.ppermute(mine, "mp", core_pairs)
    rows = POLICIES * RANK
    width = wide_a + wide_b + 128
    scratch = [VMEM((2, 2 * RANK, half), F32), VMEM((2, 2, rows, half), BF16)]
    total = ((rows, wide_a + wide_b), F32)
    (own,) = call(own_kernel, [total], [VMEM] * 4, scratch)(owner, mine, acts, cot)
    (pieces,) = call(
        grad_kernel,
        [((4, rows // 4 * (wide_a + wide_b) // 128 + 16, 128), I16)],
        [VMEM] * 5,
        scratch + [VMEM(*total)],
    )(owner, other, acts, cot, own)
    got = lax.all_to_all(pieces, BOTH, 0, 0, tiled=True, axis_index_groups=first)
    (pieces,) = call(
        functools.partial(second_kernel, wide_a, wide_b), [((4, rows // 16, width), I16)], [VMEM]
    )(got)
    got = lax.all_to_all(pieces, BOTH, 0, 0, tiled=True, axis_index_groups=second)
    deep = 4 * (wide_a + wide_b) // 128 + 4
    (pieces,) = call(
        functools.partial(third_kernel, wide_a, wide_b), [((NEAR, 2 * deep, 128), I16)], [VMEM], [VMEM((rows // 16 * (wide_a + wide_b) // 128, 128), F32)]
    )(got)
    got = lax.all_to_all(pieces, BOTH, 0, 0, tiled=True, axis_index_groups=third)
    part, packed = call(
        functools.partial(fourth_kernel, wide_a, wide_b),
        [((deep, 128), F32), ((deep + 8, 128), I16)],
        [VMEM],
    )(got)
    count = lax.axis_size("dp")
    got = lax.ppermute(packed, "dp", [(i, (i + count // 2) % count) for i in range(count)])
    return tuple(
        call(
            functools.partial(last_kernel, wide_a, wide_b), [((4, wide_a), F32), ((4, wide_b), F32)], [VMEM] * 2
        )(part, got)
    )


def solution(mesh):
    return jax.shard_map(
        shards,
        mesh=mesh,
        in_specs=(
            P("dp", "mp"),
            P("dp", "mp"),
            P("dp", None),
            P("dp", None),
            P("dp", None),
            P("dp"),
            P("dp"),
            P("mp", None),
            P(None, "mp"),
        ),
        out_specs=(P("dp", "mp"), P("dp", "mp")),
        check_vma=False,
    )
```
